256 devices in a mesh: ctx: 64 (over x_lo, y, z), tp: 4 (over x_hi, core).
Axes of the slice: x: 4 (x_hi: 2, x_lo: 2; x = x_hi * 2 + x_lo), y: 4, z: 8, core: 2. Of those that a mesh axis runs over, the one named last changes fastest.
Arguments:
- queries: bfloat16 [8192, 1024], P('ctx', 'tp'), may hold values from -18 to 18
- keys: bfloat16 [8192, 1024], P('ctx', 'tp'), may hold values from -18 to 18
- values: bfloat16 [8192, 1024], P('ctx', 'tp'), may hold values from -6 to 6
- out_grad: bfloat16 [8192, 2048], P('ctx'), may hold values from -16 to 16
- w_out: bfloat16 [1024, 2048], P('tp'), may hold values from -0.1875 to 0.1875
- frame_index: int32 [8192], replicated, may hold values from 0 to 31, as said below
- group_order: int32 [128], replicated, may hold values from 0 to 127, as said below
Outputs:
- grad_queries: bfloat16 [8192, 1024], P('ctx', 'tp')
- grad_keys: bfloat16 [8192, 1024], P('ctx', 'tp')
- grad_values: bfloat16 [8192, 1024], P('ctx', 'tp')
- grad_w_out: float32 [1024, 2048], P('tp', 'ctx')
The draws below stay inside these ranges and needn't reach their ends.
Inputs may be any that keep to these rules, and one draw needn't show every extreme that they name: `frame_index`: nondecreasing along the sequence, every frame holds one or more tokens. `group_order`: each group number appears once.
All inputs are finite; a program needn't handle non-finite values.
Results may differ from the reference program's by a relative error of at most 0.03.
Values may be sent and summed in bfloat16 or wider, within the bound.
A program may use at most 128 MiB of HBM per device.

```python
import math
import jax
import jax.numpy as jnp
from jax import lax

D = 2048
HEADS = 8
HD = 128
TOK_DEV = 128
HH = 1024
TOKENS = 8192
CH = 64
GROUPS = 128
FRAMES = 32


def row_factor(key, spread):
    return jnp.exp(jax.random.uniform(key, (TOKENS, 1), jnp.float32, -spread, spread))


def layout(key):
    group_order = jax.random.permutation(jax.random.fold_in(key, 201), GROUPS).astype(jnp.int32)
    frame_cuts = jax.random.permutation(jax.random.fold_in(key, 202), TOKENS - 1)[:FRAMES - 1] + 1
    frame_cuts = jnp.sort(frame_cuts.astype(jnp.int32)).astype(jnp.int32)
    positions = jnp.arange(TOKENS, dtype=jnp.int32)
    frame_index = jnp.sum((frame_cuts[None, :] <= positions[:, None]).astype(jnp.int32), axis=1).astype(jnp.int32)
    return (group_order, frame_index, frame_cuts)


def draw_frame_index(key, part):
    group_order, frame_index, frame_cuts = layout(key)
    return frame_index


def draw_group_order(key, part):
    group_order, frame_index, frame_cuts = layout(key)
    return group_order


def draw_out_grad(key, part):
    group_order, frame_index, frame_cuts = layout(key)
    key = jax.random.fold_in(key, 7)
    frame_starts = jnp.concatenate([jnp.zeros((1,), jnp.int32), frame_cuts])
    frame_ends = jnp.concatenate([frame_cuts, jnp.full((1,), TOKENS, jnp.int32)])
    stored = jnp.arange(TOKENS, dtype=jnp.int32)
    position = group_order[stored // CH] * CH + stored % CH
    token_frame = frame_index[position]
    within = position - frame_starts[token_frame]
    length = frame_ends[token_frame] - frame_starts[token_frame]
    twice_within = 2 * within + 1
    half_sign = jnp.where(twice_within < length, 1.0, jnp.where(twice_within > length, -1.0, 0.0)).astype(jnp.float32)
    direction = jnp.clip(jax.random.normal(jax.random.fold_in(key, 11), (D,), jnp.float32), -2.5, 2.5)
    own_noise = jnp.clip(jax.random.normal(jax.random.fold_in(key, 12), (TOKENS, D), jnp.float32), -4.0, 4.0)
    blocks = TOKENS // TOK_DEV
    pairing = jax.random.permutation(jax.random.fold_in(key, 13), blocks).astype(jnp.int32)
    row_block = stored // TOK_DEV
    col_block = jnp.arange(D, dtype=jnp.int32) // (D // blocks)
    spiked = pairing[row_block][:, None] == col_block[None, :]
    own_noise = own_noise * jnp.where(spiked, 3.0, 1.0)
    combined = 5.0 * half_sign[:, None] * direction[None, :] + own_noise
    return jnp.clip(combined, -16.0, 16.0).astype(jnp.bfloat16)


def draw_queries(key, part):
    key = jax.random.fold_in(key, 3)
    own = jax.random.normal(key, (TOKENS, HEADS * HD), jnp.float32)
    own = 0.45 * own * row_factor(jax.random.fold_in(key, 5), 0.35)
    return jnp.clip(own, -18.0, 18.0).astype(jnp.bfloat16)


def draw_keys(key, part):
    key = jax.random.fold_in(key, 4)
    own = jax.random.normal(key, (TOKENS, HEADS * HD), jnp.float32)
    own = own * row_factor(jax.random.fold_in(key, 6), 0.35)
    return jnp.clip(own, -18.0, 18.0).astype(jnp.bfloat16)


def levels(rng, dims, split, least, top_value):
    gain = 1.0
    for dim, blocks in split:
        heights = jax.random.uniform(jax.random.fold_in(jax.random.fold_in(rng, 6), dim), (blocks,), jnp.float32, least / len(split), top_value / len(split))
        gain = gain * jnp.repeat(jnp.exp(heights), dims[dim] // blocks).reshape((-1,) + (1,) * (len(dims) - 1 - dim))
    return gain


def bell_draw(stream_key, dims, scale, bound, shards=(), held_as=jnp.bfloat16):
    values = scale * jax.random.normal(stream_key, dims, jnp.float32)
    if shards:
        values = values * levels(stream_key, dims, shards, -0.22, 0.18)
    return jnp.clip(values, -bound, bound).astype(held_as)


def setup_inputs(seed: int = 0) -> dict:
    arg_keys = jax.random.split(jax.random.key(seed), 8)
    return {
        "queries": draw_queries(jax.random.fold_in(arg_keys[7], 71), 0),
        "keys": draw_keys(jax.random.fold_in(arg_keys[7], 71), 0),
        "values": bell_draw(arg_keys[2], (TOKENS, HH), 1.0, 6.0, ((0, 64), (1, 4))),
        "out_grad": draw_out_grad(jax.random.fold_in(arg_keys[7], 71), 0),
        "w_out": bell_draw(arg_keys[4], (HH, D), HH ** -0.5, 0.1875, ((0, 4),)),
        "frame_index": draw_frame_index(jax.random.fold_in(arg_keys[7], 71), 0),
        "group_order": draw_group_order(jax.random.fold_in(arg_keys[7], 71), 0),
    }


masked_score = -1.0e30


def stored_frames(frame_index, group_order):
    stored = jnp.arange(TOKENS, dtype=jnp.int32)
    position = group_order[stored // CH] * CH + stored % CH
    return frame_index[position.astype(jnp.int32)]


def block_scores(query_block, key_heads, query_frames, key_frames):
    scores = jnp.einsum("qhd,khd->hqk", query_block.astype(jnp.float32), key_heads.astype(jnp.float32)) * (HD ** -0.5)
    allowed = key_frames[None, :] <= query_frames[:, None]
    return jnp.where(allowed[None], scores, masked_score), allowed


def reference(queries, keys, values, out_grad, w_out, frame_index, group_order):
    frames = stored_frames(frame_index, group_order)
    d_attn = jnp.dot(out_grad, w_out.T, preferred_element_type=jnp.float32).astype(jnp.bfloat16)
    query_heads = queries.reshape(TOKENS, HEADS, HD)
    key_heads = keys.reshape(TOKENS, HEADS, HD)
    value_heads = values.reshape(TOKENS, HEADS, HD)
    grad_heads = d_attn.reshape(TOKENS, HEADS, HD)
    block_rows = math.gcd(TOKENS, 512)
    block_count = TOKENS // block_rows

    def forward_block(block_index):
        first_row = block_index * block_rows
        query_block = lax.dynamic_slice_in_dim(query_heads, first_row, block_rows, 0)
        query_frames = lax.dynamic_slice_in_dim(frames, first_row, block_rows, 0)
        scores, allowed = block_scores(query_block, key_heads, query_frames, frames)
        row_max = jnp.max(scores, axis=-1)
        weights = jnp.where(allowed[None], jnp.exp(scores - row_max[:, :, None]), 0.0)
        row_total = jnp.sum(weights, axis=-1)
        weights_low = weights.astype(jnp.bfloat16)
        attended = jnp.einsum("hqk,khd->qhd", weights_low.astype(jnp.float32), value_heads.astype(jnp.float32), precision=lax.Precision.HIGHEST)
        attended = attended / jnp.transpose(row_total)[:, :, None]
        return attended, row_max + jnp.log(row_total)

    attended, log_total = lax.map(forward_block, jnp.arange(block_count, dtype=jnp.int32))
    attended = attended.reshape(TOKENS, HEADS * HD).astype(jnp.bfloat16)
    log_total = jnp.transpose(log_total, (0, 2, 1)).reshape(TOKENS, HEADS)
    delta = jnp.sum((d_attn.astype(jnp.float32) * attended.astype(jnp.float32)).reshape(TOKENS, HEADS, HD), axis=-1)

    def backward_block(sums, block_index):
        first_row = block_index * block_rows
        query_block = lax.dynamic_slice_in_dim(query_heads, first_row, block_rows, 0)
        grad_block = lax.dynamic_slice_in_dim(grad_heads, first_row, block_rows, 0)
        query_frames = lax.dynamic_slice_in_dim(frames, first_row, block_rows, 0)
        log_block = lax.dynamic_slice_in_dim(log_total, first_row, block_rows, 0)
        delta_block = lax.dynamic_slice_in_dim(delta, first_row, block_rows, 0)
        scores, allowed = block_scores(query_block, key_heads, query_frames, frames)
        probs = jnp.exp(scores - jnp.transpose(log_block)[:, :, None])
        probs_low = probs.astype(jnp.bfloat16)
        grad_probs = jnp.einsum("qhd,khd->hqk", grad_block.astype(jnp.float32), value_heads.astype(jnp.float32))
        grad_scores = (probs * (grad_probs - jnp.transpose(delta_block)[:, :, None])).astype(jnp.bfloat16)
        grad_query = jnp.einsum("hqk,khd->qhd", grad_scores.astype(jnp.float32), key_heads.astype(jnp.float32))
        key_sum = sums[0] + jnp.einsum("hqk,qhd->khd", grad_scores.astype(jnp.float32), query_block.astype(jnp.float32))
        value_sum = sums[1] + jnp.einsum("hqk,qhd->khd", probs_low.astype(jnp.float32), grad_block.astype(jnp.float32))
        return (key_sum, value_sum), grad_query

    zero_rows = jnp.zeros((TOKENS, HEADS, HD), jnp.float32)
    (key_sum, value_sum), query_sum = lax.scan(backward_block, (zero_rows, zero_rows), jnp.arange(block_count, dtype=jnp.int32))
    score_scale = HD ** -0.5
    grad_queries = (query_sum.reshape(TOKENS, HEADS * HD) * score_scale).astype(jnp.bfloat16)
    grad_keys = (key_sum.reshape(TOKENS, HEADS * HD) * score_scale).astype(jnp.bfloat16)
    grad_values = value_sum.reshape(TOKENS, HEADS * HD).astype(jnp.bfloat16)
    grad_w_out = jnp.dot(attended.T, out_grad, preferred_element_type=jnp.float32)
    return (grad_queries, grad_keys, grad_values, grad_w_out)
```

```python
import functools
import math

import jax
import jax.numpy as jnp
from jax import lax
from jax.experimental import pallas as pl
from jax.experimental.pallas import tpu as pltpu
from jax.sharding import PartitionSpec as P

HD = 128
T = 128
B = 2 * T
MASKED = -1e30
FLOOR = -1e29
SCALE = HD**-0.5
EXP2_SCALE = SCALE * math.log2(math.e)
F32 = jnp.float32
BF16 = jnp.bfloat16
NT = (((1,), (1,)), ((), ()))
TN = (((0,), (0,)), ((), ()))
MESH = pl.DeviceIdType.MESH


def dot(a, b):
    return jnp.dot(a, b, preferred_element_type=F32)


def dot_general(a, b, dims):
    return lax.dot_general(a, b, dims, preferred_element_type=F32)


def kernel(
    ny,
    nz,
    q_hbm,
    k_hbm,
    v_hbm,
    og_hbm,
    w_hbm,
    fi_hbm,
    go_hbm,
    gq_ref,
    gk_ref,
    gv_ref,
    gw_ref,
    q_in,
    k_in,
    v_in,
    og_in,
    w_in,
    fi_in,
    go_in,
    da,
    kv,
    qd,
    frames,
    kf,
    qf,
    wts,
    dps,
    obuf,
    mst,
    lst,
    dst,
    stats,
    cst,
    dlt,
    osend,
    orecv,
    att,
    ogb,
    gsend,
    grecv,
    acc_k,
    acc_v,
    acc_q,
    rsk_out,
    rsk_in,
    rsv_out,
    rsv_in,
    qsend,
    qrecv,
    fin_out,
    fin_in,
    in_sem,
    xs_s,
    xs_r,
    z_s,
    z_r,
    y_s,
    y_r,
    og_s,
    og_r,
    st_s,
    st_r,
    o_s,
    o_r,
    att_s,
    att_r,
    g_s,
    g_r,
    rs_s,
    rs_r,
    dq_s,
    dq_r,
    fin_s,
    fin_r,
):
    half = nz // 2
    me = lax.axis_index("ctx")
    x = me // (ny * nz)
    y = lax.rem(me // nz, ny)
    z = lax.rem(me, nz)
    px = 1 - x
    cols = og_in.shape[1] // (2 * ny)
    zcols = cols // nz

    def at(xx, yy, zz):
        return xx * (ny * nz) + yy * nz + zz

    partner = at(px, y, z)
    right = at(x, y, lax.rem(z + 1, nz))
    left = at(x, y, lax.rem(z + nz - 1, nz))
    ypos = [lax.rem(y + k, ny) for k in range(ny)]
    ypeer = [at(x, ypos[k], z) for k in range(ny)]
    ydiag = [at(px, ypos[k], z) for k in range(ny)]
    zpos = [lax.rem(z + k, nz) for k in range(nz)]
    zpeer = [at(x, y, zpos[k]) for k in range(nz)]

    started = []

    def send(src, dst_ref, s_sem, r_sem, device):
        copy = pltpu.make_async_remote_copy(
            src_ref=src,
            dst_ref=dst_ref,
            send_sem=s_sem,
            recv_sem=r_sem,
            device_id={"ctx": device},
            device_id_type=MESH,
        )
        copy.start()
        started.append(copy)

    def arrived(dst_ref, s_sem, r_sem, device):
        pltpu.make_async_remote_copy(
            src_ref=dst_ref,
            dst_ref=dst_ref,
            send_sem=s_sem,
            recv_sem=r_sem,
            device_id={"ctx": device},
            device_id_type=MESH,
        ).wait_recv()

    loads = [
        pltpu.make_async_copy(src, to, in_sem.at[i])
        for i, (src, to) in enumerate(
            [
                (og_hbm, og_in),
                (w_hbm, w_in),
                (k_hbm, k_in),
                (v_hbm, v_in),
                (q_hbm, q_in),
                (fi_hbm, fi_in),
                (go_hbm, go_in),
            ]
        )
    ]
    for load in loads:
        load.start()
    barrier = pltpu.get_barrier_semaphore()
    peers = [partner] + ypeer[1:] + ydiag[1:] + zpeer[1:]
    for peer in peers:
        pl.semaphore_signal(barrier, inc=1, device_id={"ctx": peer}, device_id_type=MESH)
    for load in loads:
        load.wait()

    own_lanes = pl.ds(pl.multiple_of(x * HD, HD), HD)
    other_lanes = pl.ds(pl.multiple_of(px * HD, HD), HD)

    da[...] = dot_general(og_in[...], w_in[...], NT).astype(BF16)
    kv[0, 0, 0] = k_in[:, own_lanes]
    kv[0, 0, 1] = v_in[:, own_lanes]
    qd[y, 0, 0] = q_in[:, own_lanes]
    qd[y, 0, 1] = da[:, own_lanes]
    pl.semaphore_wait(barrier, len(peers))

    swap_from = [k_in, v_in, q_in, da]

    def swap_to(i):
        return kv.at[0, 1, i] if i < 2 else qd.at[y, 1, i - 2]

    for i in range(4):
        send(swap_from[i].at[:, other_lanes], swap_to(i), xs_s.at[i], xs_r.at[i], partner)

    def swapped(i):
        arrived(swap_to(i), xs_s.at[i], xs_r.at[i], partner)

    def left_slot(s):
        return s if s < half else nz - 1

    def right_slot(s):
        return half - 1 + s if s < half else nz - 1

    def z_send_right(s, c):
        source = 0 if s == 1 else left_slot(s - 1)
        slot = left_slot(s)
        send(kv.at[source, c], kv.at[slot, c], z_s.at[0, s - 1, c], z_r.at[slot, c], right)

    def z_send_left(s, c):
        source = 0 if s == 1 else right_slot(s - 1)
        slot = right_slot(s)
        send(kv.at[source, c], kv.at[slot, c], z_s.at[1, s - 1, c], z_r.at[slot, c], left)

    def z_arrived(slot, c):
        arrived(kv.at[slot, c], z_s.at[0, 0, 0], z_r.at[slot, c], left)

    def y_send(c):
        for k in range(1, ny):
            r = ny - k
            send(qd.at[y, c], qd.at[y, c], y_s.at[k, c], y_r.at[r, c], ypeer[k])

    z_send_right(1, 0)
    z_send_left(1, 0)
    y_send(0)

    go = go_in[...]
    fi = fi_in[...].astype(F32)
    pairs, lanes = fi.shape
    groups = go.shape[1]
    half_lanes = lanes // 2
    lane = lax.broadcasted_iota(jnp.int32, (pairs, lanes), 1)
    low = jnp.where(lane < half_lanes, fi, 0.0)
    high = jnp.where(lane >= half_lanes, fi, 0.0)
    low_up = jnp.concatenate([low[:, half_lanes:], low[:, :half_lanes]], axis=1)
    high_down = jnp.concatenate([high[:, half_lanes:], high[:, :half_lanes]], axis=1)
    row = lax.broadcasted_iota(jnp.int32, (pairs, groups), 0)
    holds = [(go == 2 * row + p).astype(F32).astype(BF16) for p in range(2)]
    group_id = lax.broadcasted_iota(jnp.int32, (groups, pairs), 0)
    pair_id = lax.broadcasted_iota(jnp.int32, (groups, pairs), 1)
    picks = [(group_id == 2 * pair_id + e).astype(F32).astype(BF16) for e in range(2)]
    total = jnp.zeros((pairs, lanes), F32)
    for p in range(2):
        for e in range(2):
            part = ((low, low_up), (high_down, high))[p][e]
            total += dot_general(dot(holds[p], picks[e]).astype(BF16), part.astype(BF16), TN)
    frames[...] = total
    across = jnp.transpose(total)
    device_lane = lax.broadcasted_iota(jnp.int32, (lanes, pairs), 1)
    distance = (
        [0] + [nz - s for s in range(1, half)] + [s for s in range(1, half)] + [half]
    )
    for slot in range(nz):
        for c in range(2):
            source = at(x if c == 0 else px, y, zpos[distance[slot]])
            column = jnp.sum(jnp.where(device_lane == source, across, 0.0), axis=1, keepdims=True)
            kf[slot, pl.ds(c * T, T), :] = jnp.broadcast_to(column, (T, lanes))
    for b in range(ny):
        qf[pl.ds(b, 1), pl.ds(0, T)] = frames[pl.ds(at(x, b, z), 1), :]
        qf[pl.ds(b, 1), pl.ds(T, T)] = frames[pl.ds(at(px, b, z), 1), :]

    swapped(0)
    swapped(1)
    z_send_right(1, 1)
    z_send_left(1, 1)
    swapped(2)
    swapped(3)
    y_send(1)

    def og_lanes(xx, yy):
        return pl.ds(pl.multiple_of((xx * ny + yy) * cols, cols), cols)

    og_targets = [(x, k, ypeer[k]) for k in range(1, ny)] + [(px, k, ydiag[k]) for k in range(ny)]

    def og_send():
        ogb[y, x] = og_in[:, og_lanes(x, y)]
        for i, (xx, k, device) in enumerate(og_targets):
            side = 0 if i < ny - 1 else 1
            r = (ny - k) % ny
            send(
                og_in.at[:, og_lanes(xx, ypos[k])],
                ogb.at[y, x],
                og_s.at[i],
                og_r.at[side, r],
                device,
            )

    def forward(slot):
        kb = kv[slot, :, 0].reshape(B, HD)
        vb = kv[slot, :, 1].reshape(B, HD)
        v_t = jnp.transpose(vb)
        key_frames = jnp.concatenate([kf[slot], kf[slot]], axis=1)

        def body(b, carry):
            scores = dot_general(kb, qd[b, :, 0].reshape(B, HD), NT)
            grads = dot_general(vb, qd[b, :, 1].reshape(B, HD), NT)
            scores = jnp.where(key_frames <= qf[pl.ds(b, 1), :], scores, MASKED)
            top = jnp.maximum(jnp.max(scores, axis=0, keepdims=True), FLOOR)
            weights = jnp.exp2((scores - top) * EXP2_SCALE)
            wts[slot, b] = weights
            dps[slot, b] = grads
            mst[slot, pl.ds(b, 1), :] = top
            lst[slot, pl.ds(b, 1), :] = jnp.sum(weights, axis=0, keepdims=True)
            dst[slot, pl.ds(b, 1), :] = jnp.sum(weights * grads, axis=0, keepdims=True)
            obuf[slot, b] = dot(v_t, weights.astype(BF16))
            return carry

        lax.fori_loop(0, ny, body, 0)

    def relay(s, c):
        z_arrived(left_slot(s), c)
        if s + 1 < half or (s + 1 == half and c == 0):
            z_send_right(s + 1, c)
        z_arrived(right_slot(s), c)
        if s + 1 < half or (s + 1 == half and c == 1):
            z_send_left(s + 1, c)

    relay(1, 0)
    relay(1, 1)
    for c in range(2):
        for k in range(1, ny):
            arrived(qd.at[ypos[k], c], y_s.at[k, c], y_r.at[k, c], ypeer[k])
    og_send()
    forward(0)
    for s in range(1, half):
        if s + 1 < half:
            forward(left_slot(s))
            relay(s + 1, 0)
            forward(right_slot(s))
            relay(s + 1, 1)
        else:
            forward(left_slot(s))
            forward(right_slot(s))
    z_arrived(nz - 1, 0)
    z_arrived(nz - 1, 1)
    forward(nz - 1)

    tops = mst[...]
    own_top = jnp.max(tops, axis=0)
    shares = jnp.exp2((tops - own_top[None]) * EXP2_SCALE)
    stats[y, 0] = own_top
    stats[y, 1] = jnp.sum(shares * lst[...], axis=0)
    stats[y, 2] = jnp.sum(shares * dst[...], axis=0)
    for k in range(1, ny):
        send(stats.at[y], stats.at[y], st_s.at[k], st_r.at[ny - k], ypeer[k])
    for k in range(1, ny):
        arrived(stats.at[ypos[k]], st_s.at[k], st_r.at[k], ypeer[k])
    all_top = stats[0, 0]
    for b in range(1, ny):
        all_top = jnp.maximum(all_top, stats[b, 0])
    row_total = jnp.zeros_like(all_top)
    delta = jnp.zeros_like(all_top)
    for b in range(ny):
        share = jnp.exp2((stats[b, 0] - all_top) * EXP2_SCALE)
        row_total += share * stats[b, 1]
        delta += share * stats[b, 2]
    inverse = 1.0 / row_total
    dlt[...] = delta * inverse
    cst[...] = jnp.exp2((tops - all_top[None]) * EXP2_SCALE) * inverse[None]

    def attended_part(b, carry):
        part = obuf[0, b] * cst[0, pl.ds(b, 1), :]
        for slot in range(1, nz):
            part += obuf[slot, b] * cst[slot, pl.ds(b, 1), :]
        osend[b] = part.astype(BF16)
        return carry

    lax.fori_loop(0, ny, attended_part, 0)
    for k in range(1, ny):
        send(osend.at[ypos[k]], orecv.at[ny - k], o_s.at[k], o_r.at[ny - k], ypeer[k])

    acc_q[...] = jnp.zeros_like(acc_q)

    def backward(slot):
        k_t = jnp.transpose(kv[slot, :, 0].reshape(B, HD))
        acc_k[...] = jnp.zeros_like(acc_k)
        acc_v[...] = jnp.zeros_like(acc_v)

        def body(b, carry):
            probs = wts[slot, b] * cst[slot, pl.ds(b, 1), :]
            grad_scores = (probs * (dps[slot, b] - dlt[pl.ds(b, 1), :])).astype(BF16)
            acc_v[...] += dot(probs.astype(BF16), qd[b, :, 1].reshape(B, HD))
            acc_k[...] += dot(grad_scores, qd[b, :, 0].reshape(B, HD))
            acc_q[b] += dot(k_t, grad_scores)
            return carry

        lax.fori_loop(0, ny, body, 0)

    def reduce_arrived(way, step, c):
        i = step - 1
        for t, to in enumerate((rsv_in, rsk_in)):
            arrived(to.at[way, i, c], rs_s.at[t, way, i, c], rs_r.at[t, way, i, c], left)
        return rsk_in[way, i, c].astype(F32), rsv_in[way, i, c]

    def reduce_send(way, step, c, arrival):
        part_k = acc_k[pl.ds(c * T, T), :]
        part_v = acc_v[pl.ds(c * T, T), :]
        if arrival:
            more_k, more_v = reduce_arrived(way, step - 1, c)
            part_k += more_k
            part_v += more_v
        i = step - 1
        rsk_out[way, i, c] = part_k.astype(BF16)
        rsv_out[way, i, c] = part_v
        device = right if way == 0 else left
        for t, (src, to) in enumerate(((rsv_out, rsv_in), (rsk_out, rsk_in))):
            send(src.at[way, i, c], to.at[way, i, c], rs_s.at[t, way, i, c], rs_r.at[t, way, i, c], device)

    backward(nz - 1)
    reduce_send(0, 1, 0, False)
    reduce_send(1, 1, 1, False)

    for k in range(1, ny):
        arrived(orecv.at[k], o_s.at[k], o_r.at[k], ypeer[k])
    rows_att = osend[y].astype(F32)
    for k in range(1, ny):
        rows_att += orecv[k].astype(F32)
    att[x, y] = rows_att.astype(BF16)
    for i, (xx, k, device) in enumerate(og_targets):
        side = 0 if i < ny - 1 else 1
        send(att.at[x, y], att.at[x, y], att_s.at[i], att_r.at[side, (ny - k) % ny], device)

    def reduce_step(step):
        d = half + 1 - step
        backward(right_slot(d))
        for c in range(2):
            reduce_send(0, step, c, step > 2 or c == 0)
        backward(left_slot(d))
        for c in range(2):
            reduce_send(1, step, c, step > 2 or c == 1)

    reduce_step(2)

    for i, (xx, k, device) in enumerate(og_targets):
        side = 0 if i < ny - 1 else 1
        source_x = x if side == 0 else px
        arrived(ogb.at[ypos[k], source_x], og_s.at[i], og_r.at[side, k], device)
        arrived(att.at[source_x, ypos[k]], att_s.at[i], att_r.at[side, k], device)
    for h in range(2):
        part = jnp.zeros((HD, cols), F32)
        for b in range(ny):
            for c in range(2):
                part += dot(att[h, b, :, pl.ds(c * T, T)], ogb[b, h ^ c])
        gsend[:, :, pl.ds(h * HD, HD)] = jnp.transpose(part).reshape(nz, zcols, HD)
    for k in range(1, nz):
        send(gsend.at[zpos[k]], grecv.at[nz - k], g_s.at[k], g_r.at[nz - k], zpeer[k])

    for step in range(3, half + 1):
        reduce_step(step)
    backward(0)

    for b in range(ny):
        qsend[b] = acc_q[b].astype(BF16)
    for k in range(1, ny):
        send(qsend.at[ypos[k]], qrecv.at[ny - k], dq_s.at[k], dq_r.at[ny - k], ypeer[k])

    for k in range(1, nz):
        arrived(grecv.at[k], g_s.at[k], g_r.at[k], zpeer[k])
    weight_rows = gsend[z]
    for k in range(1, nz):
        weight_rows += grecv[k]
    gw_ref[...] = jnp.transpose(weight_rows)

    for c in (1, 0):
        part_k = acc_k[pl.ds(c * T, T), :]
        part_v = acc_v[pl.ds(c * T, T), :]
        for way in range(2):
            more_k, more_v = reduce_arrived(way, half, c)
            part_k += more_k
            part_v += more_v
        out_k = (part_k * SCALE).astype(BF16)
        out_v = part_v.astype(BF16)
        if c == 1:
            fin_out[0] = out_k
            fin_out[1] = out_v
            for i in range(2):
                send(fin_out.at[i], fin_in.at[i], fin_s.at[i], fin_r.at[i], partner)
        else:
            gk_ref[:, own_lanes] = out_k
            gv_ref[:, own_lanes] = out_v

    for k in range(1, ny):
        arrived(qrecv.at[k], dq_s.at[k], dq_r.at[k], ypeer[k])
    query_rows = acc_q[y]
    for k in range(1, ny):
        query_rows += qrecv[k].astype(F32)
    out_q = jnp.transpose(query_rows * SCALE).astype(BF16)
    fin_out[2] = out_q[T:]
    send(fin_out.at[2], fin_in.at[2], fin_s.at[2], fin_r.at[2], partner)
    gq_ref[:, own_lanes] = out_q[:T]
    for i, ref in enumerate((gk_ref, gv_ref, gq_ref)):
        arrived(fin_in.at[i], fin_s.at[i], fin_r.at[i], partner)
        ref[:, other_lanes] = fin_in[i]

    for copy in started:
        copy.wait_send()


def shards(ny, nz, queries, keys, values, out_grad, w_out, frame_index, group_order):
    half = nz // 2
    width = out_grad.shape[1]
    cols = width // (2 * ny)
    zcols = cols // nz
    pairs = group_order.shape[0] // 2
    frames_in = frame_index.reshape(pairs, T)
    order_in = group_order.reshape(1, 2 * pairs)
    vmem = pltpu.VMEM
    dma = pltpu.SemaphoreType.DMA
    any_spec = pl.BlockSpec(memory_space=pl.ANY)
    out_spec = pl.BlockSpec(memory_space=pltpu.VMEM)
    plane = 2 * ny - 1
    return pl.pallas_call(
        functools.partial(kernel, ny, nz),
        out_shape=(
            jax.ShapeDtypeStruct((T, 2 * HD), BF16),
            jax.ShapeDtypeStruct((T, 2 * HD), BF16),
            jax.ShapeDtypeStruct((T, 2 * HD), BF16),
            jax.ShapeDtypeStruct((2 * HD, zcols), F32),
        ),
        in_specs=[any_spec] * 7,
        out_specs=(out_spec,) * 4,
        scratch_shapes=[
            vmem((T, 2 * HD), BF16),
            vmem((T, 2 * HD), BF16),
            vmem((T, 2 * HD), BF16),
            vmem((T, width), BF16),
            vmem((2 * HD, width), BF16),
            vmem((pairs, T), jnp.int32),
            vmem((1, 2 * pairs), jnp.int32),
            vmem((T, 2 * HD), BF16),
            vmem((nz, 2, 2, T, HD), BF16),
            vmem((ny, 2, 2, T, HD), BF16),
            vmem((pairs, T), F32),
            vmem((nz, B, T), F32),
            vmem((ny, B), F32),
            vmem((nz, ny, B, B), F32),
            vmem((nz, ny, B, B), F32),
            vmem((nz, ny, HD, B), F32),
            vmem((nz, ny, B), F32),
            vmem((nz, ny, B), F32),
            vmem((nz, ny, B), F32),
            vmem((ny, 3, ny, B), F32),
            vmem((nz, ny, B), F32),
            vmem((ny, B), F32),
            vmem((ny, HD, B), BF16),
            vmem((ny, HD, B), BF16),
            vmem((2, ny, HD, B), BF16),
            vmem((ny, 2, T, cols), BF16),
            vmem((nz, zcols, 2 * HD), F32),
            vmem((nz, zcols, 2 * HD), F32),
            vmem((B, HD), F32),
            vmem((B, HD), F32),
            vmem((ny, HD, B), F32),
            vmem((2, half, 2, T, HD), BF16),
            vmem((2, half, 2, T, HD), BF16),
            vmem((2, half, 2, T, HD), F32),
            vmem((2, half, 2, T, HD), F32),
            vmem((ny, HD, B), BF16),
            vmem((ny, HD, B), BF16),
            vmem((3, T, HD), BF16),
            vmem((3, T, HD), BF16),
            dma((7,)),
            dma((4,)),
            dma((4,)),
            dma((2, half, 2)),
            dma((nz, 2)),
            dma((ny, 2)),
            dma((ny, 2)),
            dma((plane,)),
            dma((2, ny)),
            dma((ny,)),
            dma((ny,)),
            dma((ny,)),
            dma((ny,)),
            dma((plane,)),
            dma((2, ny)),
            dma((nz,)),
            dma((nz,)),
            dma((2, 2, half, 2)),
            dma((2, 2, half, 2)),
            dma((ny,)),
            dma((ny,)),
            dma((3,)),
            dma((3,)),
        ],
        compiler_params=pltpu.CompilerParams(
            collective_id=0, has_side_effects=True, vmem_limit_bytes=50 * 1024 * 1024
        ),
    )(queries, keys, values, out_grad, w_out, frames_in, order_in)


def solution(mesh):
    ny, nz = {64: (4, 8), 16: (2, 4)}[mesh.shape["ctx"]]
    placed = (
        P("ctx", "tp"),
        P("ctx", "tp"),
        P("ctx", "tp"),
        P("ctx", None),
        P("tp", None),
        P(),
        P(),
    )
    return jax.shard_map(
        functools.partial(shards, ny, nz),
        mesh=mesh,
        in_specs=placed,
        out_specs=(P("ctx", "tp"), P("ctx", "tp"), P("ctx", "tp"), P("tp", "ctx")),
        check_vma=False,
    )
```

```python
import functools
import math

import jax
import jax.numpy as jnp
from jax import lax
from jax.experimental import pallas as pl
from jax.experimental.pallas import tpu as pltpu
from jax.sharding import PartitionSpec as P

HD = 128
T = 128
B = 2 * T
MASKED = -1e30
FLOOR = -1e29
SCALE = HD**-0.5
EXP2_SCALE = SCALE * math.log2(math.e)
F32 = jnp.float32
BF16 = jnp.bfloat16
NT = (((1,), (1,)), ((), ()))
TN = (((0,), (0,)), ((), ()))
MESH = pl.DeviceIdType.MESH


def dot(a, b):
    return jnp.dot(a, b, preferred_element_type=F32)


def dot_general(a, b, dims):
    return lax.dot_general(a, b, dims, preferred_element_type=F32)


def kernel(
    ny,
    nz,
    q_hbm,
    k_hbm,
    v_hbm,
    og_hbm,
    w_hbm,
    fi_hbm,
    go_hbm,
    gq_ref,
    gk_ref,
    gv_ref,
    gw_ref,
    q_in,
    k_in,
    v_in,
    og_in,
    w_in,
    fi_in,
    go_in,
    da,
    kv_other,
    qd_other,
    kv,
    qd,
    frames,
    kf,
    qf,
    wts,
    dps,
    obuf,
    mst,
    lst,
    dst,
    stats,
    cst,
    ysh,
    dlt,
    osend,
    orecv,
    att,
    ogb,
    gsend,
    grecv,
    acc_k,
    acc_v,
    acc_q,
    rsk_out,
    rsk_in,
    rsv_out,
    rsv_in,
    qsend,
    qrecv,
    finv_out,
    finv_in,
    fink_out,
    fink_in,
    in_sem,
    sent,
    z_r,
    y_r,
    og_r,
    st_r,
    o_r,
    att_r,
    g_r,
    rs_r,
    dq_r,
    fin_r,
):
    half = nz // 2
    me = lax.axis_index("ctx")
    x = me // (ny * nz)
    y = lax.rem(me // nz, ny)
    z = lax.rem(me, nz)
    px = 1 - x
    cols = og_in.shape[1] // (2 * ny)
    zcols = cols // nz

    def at(xx, yy, zz):
        return xx * (ny * nz) + yy * nz + zz

    partner = at(px, y, z)
    right = at(x, y, lax.rem(z + 1, nz))
    left = at(x, y, lax.rem(z + nz - 1, nz))
    ypos = [lax.rem(y + k, ny) for k in range(ny)]
    ypeer = [at(x, ypos[k], z) for k in range(ny)]
    ydiag = [at(px, ypos[k], z) for k in range(ny)]
    zpos = [lax.rem(z + k, nz) for k in range(nz)]
    zpeer = [at(x, y, zpos[k]) for k in range(nz)]
    zdiag = [at(px, y, zpos[k]) for k in range(nz)]

    started = []

    def send(src, dst_ref, r_sem, device):
        copy = pltpu.make_async_remote_copy(
            src_ref=src,
            dst_ref=dst_ref,
            send_sem=sent.at[len(started)],
            recv_sem=r_sem,
            device_id={"ctx": device},
            device_id_type=MESH,
        )
        copy.start()
        started.append(copy)

    def arrived(dst_ref, r_sem):
        pltpu.make_async_remote_copy(
            src_ref=dst_ref,
            dst_ref=dst_ref,
            send_sem=sent.at[0],
            recv_sem=r_sem,
            device_id={"ctx": partner},
            device_id_type=MESH,
        ).wait_recv()

    loads = [
        pltpu.make_async_copy(src, to, in_sem.at[i])
        for i, (src, to) in enumerate(
            [
                (k_hbm, k_in),
                (v_hbm, v_in),
                (w_hbm, w_in),
                (og_hbm, og_in),
                (q_hbm, q_in),
                (fi_hbm, fi_in),
                (go_hbm, go_in),
            ]
        )
    ]
    for load in loads:
        load.start()
    barrier = pltpu.get_barrier_semaphore()
    peers = ydiag + ypeer[1:] + zpeer[1:] + [zdiag[k] for k in sorted({1, 2, nz - 2, nz - 1})]
    for peer in peers:
        pl.semaphore_signal(barrier, inc=1, device_id={"ctx": peer}, device_id_type=MESH)
    own_lanes = pl.ds(pl.multiple_of(x * HD, HD), HD)
    other_lanes = pl.ds(pl.multiple_of(px * HD, HD), HD)

    def stage(src, own, other, i):
        own[i] = src[:, own_lanes]
        other[i] = src[:, other_lanes]

    loads[0].wait()
    loads[1].wait()
    stage(k_in, kv.at[0, 0], kv_other, 0)
    stage(v_in, kv.at[0, 0], kv_other, 1)
    pl.semaphore_wait(barrier, len(peers))

    def left_slot(s):
        return s if s < half else nz - 1

    def right_slot(s):
        return half - 1 + s if s < half else nz - 1

    reach = min(2, half - 1)

    def kv_first(distance, way, c):
        slot = (left_slot, right_slot)[way](distance)
        k = distance if way == 0 else nz - distance
        send(kv.at[0, 0] if c == 0 else kv_other, kv.at[slot, c], z_r.at[slot, c], (zpeer, zdiag)[c][k])

    for c in range(2):
        for d in range(reach, 0, -1):
            for way in range(2):
                kv_first(d, way, c)
    send(kv_other, kv.at[0, 1], z_r.at[0, 1], partner)
    if half == 2:
        kv_first(2, 0, 0)
        kv_first(2, 1, 1)

    def z_arrived(slot, c):
        arrived(kv.at[slot, c], z_r.at[slot, c])

    def pass_on(c):
        for way in range(2):
            slot = (left_slot, right_slot)[way](2)
            z_arrived(slot, c)
            for d in (3, 4):
                if d < half or (d == half and way == c):
                    to = (left_slot, right_slot)[way](d)
                    k = d - 2 if way == 0 else nz - (d - 2)
                    send(kv.at[slot, c], kv.at[to, c], z_r.at[to, c], zpeer[k])

    for load in loads[2:]:
        load.wait()
    da[...] = dot_general(og_in[...], w_in[...], NT).astype(BF16)
    stage(q_in, qd.at[y, 0], qd_other, 0)
    stage(da, qd.at[y, 0], qd_other, 1)
    for k in range(1, ny):
        send(qd.at[y, 0], qd.at[y, 0], y_r.at[ny - k, 0], ypeer[k])
    for k in range(ny):
        send(qd_other, qd.at[y, 1], y_r.at[(ny - k) % ny, 1], ydiag[k])

    go = go_in[...]
    fi = fi_in[...].astype(F32)
    pairs, lanes = fi.shape
    groups = go.shape[1]
    half_lanes = lanes // 2
    lane = lax.broadcasted_iota(jnp.int32, (pairs, lanes), 1)
    low = jnp.where(lane < half_lanes, fi, 0.0)
    high = jnp.where(lane >= half_lanes, fi, 0.0)
    low_up = jnp.concatenate([low[:, half_lanes:], low[:, :half_lanes]], axis=1)
    high_down = jnp.concatenate([high[:, half_lanes:], high[:, :half_lanes]], axis=1)
    row = lax.broadcasted_iota(jnp.int32, (pairs, groups), 0)
    holds = [(go == 2 * row + p).astype(F32).astype(BF16) for p in range(2)]
    group_id = lax.broadcasted_iota(jnp.int32, (groups, pairs), 0)
    pair_id = lax.broadcasted_iota(jnp.int32, (groups, pairs), 1)
    picks = [(group_id == 2 * pair_id + e).astype(F32).astype(BF16) for e in range(2)]
    total = jnp.zeros((pairs, lanes), F32)
    for p in range(2):
        for e in range(2):
            part = ((low, low_up), (high_down, high))[p][e]
            total += dot_general(dot(holds[p], picks[e]).astype(BF16), part.astype(BF16), TN)
    frames[...] = total
    across = jnp.transpose(total)
    device_lane = lax.broadcasted_iota(jnp.int32, (lanes, pairs), 1)
    distance = (
        [0] + [nz - s for s in range(1, half)] + [s for s in range(1, half)] + [half]
    )
    for slot in range(nz):
        for c in range(2):
            source = at(x if c == 0 else px, y, zpos[distance[slot]])
            column = jnp.sum(jnp.where(device_lane == source, across, 0.0), axis=1, keepdims=True)
            kf[slot, pl.ds(c * T, T), :] = jnp.broadcast_to(column, (T, lanes))
    for b in range(ny):
        qf[pl.ds(b, 1), pl.ds(0, T)] = frames[pl.ds(at(x, b, z), 1), :]
        qf[pl.ds(b, 1), pl.ds(T, T)] = frames[pl.ds(at(px, b, z), 1), :]

    def og_lanes(xx, yy):
        return pl.ds(pl.multiple_of((xx * ny + yy) * cols, cols), cols)

    og_targets = [(x, k, ypeer[k]) for k in range(1, ny)] + [(px, k, ydiag[k]) for k in range(ny)]

    def og_send():
        ogb[y, x] = og_in[:, og_lanes(x, y)]
        for i, (xx, k, device) in enumerate(og_targets):
            side = 0 if i < ny - 1 else 1
            r = (ny - k) % ny
            send(
                og_in.at[:, og_lanes(xx, ypos[k])],
                ogb.at[y, x],
                og_r.at[side, r],
                device,
            )

    def forward(slot):
        kb = kv[slot, :, 0].reshape(B, HD)
        vb = kv[slot, :, 1].reshape(B, HD)
        v_t = jnp.transpose(vb)
        key_frames = jnp.concatenate([kf[slot], kf[slot]], axis=1)

        def body(b, carry):
            scores = dot_general(kb, qd[b, :, 0].reshape(B, HD), NT)
            grads = dot_general(vb, qd[b, :, 1].reshape(B, HD), NT)
            scores = jnp.where(key_frames <= qf[pl.ds(b, 1), :], scores, MASKED)
            top = jnp.maximum(jnp.max(scores, axis=0, keepdims=True), FLOOR)
            weights = jnp.exp2((scores - top) * EXP2_SCALE)
            wts[slot, b] = weights
            dps[slot, b] = grads
            mst[slot, pl.ds(b, 1), :] = top
            lst[slot, pl.ds(b, 1), :] = jnp.sum(weights, axis=0, keepdims=True)
            dst[slot, pl.ds(b, 1), :] = jnp.sum(weights * grads, axis=0, keepdims=True)
            obuf[slot, b] = dot(v_t, weights.astype(BF16))
            return carry

        lax.fori_loop(0, ny, body, 0, unroll=True)

    if half > 2:
        pass_on(0)
        pass_on(1)
    z_arrived(0, 1)
    for k in range(ny):
        for c in range(2):
            if k + c > 0:
                arrived(qd.at[ypos[k], c], y_r.at[k, c])
    og_send()
    forward(0)
    for s in range(1, half):
        for slot in (left_slot(s), right_slot(s)):
            if s != 2 or half == 2:
                z_arrived(slot, 0)
                z_arrived(slot, 1)
            forward(slot)
    z_arrived(nz - 1, 0)
    z_arrived(nz - 1, 1)
    forward(nz - 1)

    tops = mst[...]
    own_top = jnp.max(tops, axis=0)
    shares = jnp.exp2((tops - own_top[None]) * EXP2_SCALE)
    stats[y, 0] = own_top
    stats[y, 1] = jnp.sum(shares * lst[...], axis=0)
    stats[y, 2] = jnp.sum(shares * dst[...], axis=0)
    for k in range(1, ny):
        send(stats.at[y], stats.at[y], st_r.at[ny - k], ypeer[k])

    cst[...] = shares

    def attended_part(b, carry):
        part = obuf[0, b] * cst[0, pl.ds(b, 1), :]
        for slot in range(1, nz):
            part += obuf[slot, b] * cst[slot, pl.ds(b, 1), :]
        osend[b] = part.astype(BF16)
        return carry

    lax.fori_loop(0, ny, attended_part, 0)
    for k in range(1, ny):
        send(osend.at[ypos[k]], orecv.at[ny - k], o_r.at[ny - k], ypeer[k])

    for k in range(1, ny):
        arrived(stats.at[ypos[k]], st_r.at[k])
    all_top = stats[0, 0]
    for b in range(1, ny):
        all_top = jnp.maximum(all_top, stats[b, 0])
    row_total = jnp.zeros_like(all_top)
    delta = jnp.zeros_like(all_top)
    for b in range(ny):
        share = jnp.exp2((stats[b, 0] - all_top) * EXP2_SCALE)
        row_total += share * stats[b, 1]
        delta += share * stats[b, 2]
        ysh[b] = share
    inverse = 1.0 / row_total
    for b in range(ny):
        ysh[b] = ysh[b] * inverse
    dlt[...] = delta * inverse
    cst[...] = jnp.exp2((tops - all_top[None]) * EXP2_SCALE) * inverse[None]

    acc_q[...] = jnp.zeros_like(acc_q)

    def backward(slot):
        k_t = jnp.transpose(kv[slot, :, 0].reshape(B, HD))
        acc_k[slot] = jnp.zeros((B, HD), F32)
        acc_v[slot] = jnp.zeros((B, HD), F32)

        def body(b, carry):
            probs = wts[slot, b] * cst[slot, pl.ds(b, 1), :]
            grad_scores = (probs * (dps[slot, b] - dlt[pl.ds(b, 1), :])).astype(BF16)
            acc_v[slot] += dot(probs.astype(BF16), qd[b, :, 1].reshape(B, HD))
            acc_k[slot] += dot(grad_scores, qd[b, :, 0].reshape(B, HD))
            acc_q[b] += dot(k_t, grad_scores)
            return carry

        lax.fori_loop(0, ny, body, 0, unroll=True)

    def reduce_send(way, step, c, arrival):
        d = half + 1 - step
        i = step - 1
        slot = (right_slot, left_slot)[way](d)
        k = 1 if way == 0 else nz - 1
        device = zdiag[k] if step == half and c == 1 else zpeer[k]
        for t, (acc, src, to) in enumerate(((acc_v, rsv_out, rsv_in), (acc_k, rsk_out, rsk_in))):
            part = acc[slot, pl.ds(c * T, T), :]
            if arrival:
                arrived(to.at[way, i - 1, c], rs_r.at[t, way, i - 1, c])
                part += to[way, i - 1, c].astype(F32)
            src[way, i, c] = part.astype(src.dtype)
            send(src.at[way, i, c], to.at[way, i, c], rs_r.at[t, way, i, c], device)

    def reduce_rest(step):
        if step > 2:
            reduce_send(0, step, 1, True)
            reduce_send(1, step, 0, True)
        reduce_send(0, step, 0, True)
        reduce_send(1, step, 1, True)

    def attended_rows():
        for k in range(1, ny):
            arrived(orecv.at[k], o_r.at[k])
        rows_att = osend[y].astype(F32) * ysh[y, pl.ds(y, 1), :]
        for k in range(1, ny):
            rows_att += orecv[k].astype(F32) * ysh[ypos[k], pl.ds(y, 1), :]
        att[x, y] = rows_att.astype(BF16)
        for i, (xx, k, device) in enumerate(og_targets):
            side = 0 if i < ny - 1 else 1
            send(att.at[x, y], att.at[x, y], att_r.at[side, (ny - k) % ny], device)

    def query_part():
        backward(0)
        for t, (acc, src, to) in enumerate(((acc_v, finv_out, finv_in), (acc_k, fink_out, fink_in))):
            src[...] = acc[0, pl.ds(T, T), :].astype(src.dtype)
            send(src, to, fin_r.at[t], partner)
        for b in range(ny):
            for c in range(2):
                qsend[b, c] = acc_q[b, :, pl.ds(c * T, T)].astype(BF16)
        for k in range(ny):
            r = (ny - k) % ny
            if k > 0:
                send(qsend.at[ypos[k], 0], qrecv.at[0, r], dq_r.at[0, r], ypeer[k])
            send(qsend.at[ypos[k], 1], qrecv.at[1, r], dq_r.at[1, r], ydiag[k])

    def weight_part():
        for i, (xx, k, device) in enumerate(og_targets):
            side = 0 if i < ny - 1 else 1
            source_x = x if side == 0 else px
            arrived(ogb.at[ypos[k], source_x], og_r.at[side, k])
            arrived(att.at[source_x, ypos[k]], att_r.at[side, k])
        for h in range(2):
            part = jnp.zeros((HD, cols), F32)
            for b in range(ny):
                for c in range(2):
                    part += dot(att[h, b, :, pl.ds(c * T, T)], ogb[b, h ^ c])
            gsend[:, :, pl.ds(h * HD, HD)] = jnp.transpose(part).reshape(nz, zcols, HD)
        for k in range(1, nz):
            send(gsend.at[zpos[k]], grecv.at[nz - k], g_r.at[nz - k], zpeer[k])

    backward(nz - 1)
    reduce_send(0, 1, 0, False)
    reduce_send(1, 1, 1, False)
    backward(right_slot(half - 1))
    reduce_send(0, 2, 1, False)
    backward(left_slot(half - 1))
    reduce_send(1, 2, 0, False)
    if half > 2:
        backward(right_slot(half - 2))
    attended_rows()
    if half > 2:
        backward(left_slot(half - 2))
    reduce_rest(2)
    for step in range(3, half + 1):
        if step < half:
            backward(right_slot(half - step))
            backward(left_slot(half - step))
        if step == half:
            query_part()
        reduce_rest(step)
        if step == 3:
            weight_part()
    if half == 2:
        query_part()
        weight_part()

    for t, (acc, src, to) in enumerate(((acc_v, finv_out, finv_in), (acc_k, fink_out, fink_in))):
        arrived(to, fin_r.at[t])
    for k in range(ny):
        for c in range(2):
            if k + c > 0:
                arrived(qrecv.at[c, k], dq_r.at[c, k])
    for c, lanes_out in enumerate((own_lanes, other_lanes)):
        rows_q = qsend[y, 0].astype(F32) if c == 0 else qrecv[1, 0].astype(F32)
        for k in range(1, ny):
            rows_q += qrecv[c, k].astype(F32)
        gq_ref[:, lanes_out] = jnp.transpose(rows_q * SCALE).astype(BF16)
    for k in range(1, nz):
        arrived(grecv.at[k], g_r.at[k])
    weight_rows = gsend[z]
    for k in range(1, nz):
        weight_rows += grecv[k]
    gw_ref[...] = weight_rows
    for c, lanes_out in ((1, other_lanes), (0, own_lanes)):
        part_v = finv_in[...] if c == 1 else acc_v[0, pl.ds(0, T), :]
        part_k = fink_in[...].astype(F32) if c == 1 else acc_k[0, pl.ds(0, T), :]
        for way in (0, 1) if c == 1 else (1, 0):
            arrived(rsv_in.at[way, half - 1, c], rs_r.at[0, way, half - 1, c])
            part_v += rsv_in[way, half - 1, c]
            arrived(rsk_in.at[way, half - 1, c], rs_r.at[1, way, half - 1, c])
            part_k += rsk_in[way, half - 1, c].astype(F32)
        gv_ref[:, lanes_out] = part_v.astype(BF16)
        gk_ref[:, lanes_out] = (part_k * SCALE).astype(BF16)

    for copy in started:
        copy.wait_send()


def shards(ny, nz, queries, keys, values, out_grad, w_out, frame_index, group_order):
    half = nz // 2
    width = out_grad.shape[1]
    cols = width // (2 * ny)
    zcols = cols // nz
    pairs = group_order.shape[0] // 2
    frames_in = frame_index.reshape(pairs, T)
    order_in = group_order.reshape(1, 2 * pairs)
    vmem = pltpu.VMEM
    dma = pltpu.SemaphoreType.DMA
    any_spec = pl.BlockSpec(memory_space=pltpu.HBM)
    out_spec = pl.BlockSpec(memory_space=pltpu.VMEM)
    results = pl.pallas_call(
        functools.partial(kernel, ny, nz),
        out_shape=(
            jax.ShapeDtypeStruct((T, 2 * HD), BF16),
            jax.ShapeDtypeStruct((T, 2 * HD), BF16),
            jax.ShapeDtypeStruct((T, 2 * HD), BF16),
            jax.ShapeDtypeStruct((zcols, 2 * HD), F32),
        ),
        in_specs=[any_spec] * 7,
        out_specs=(out_spec,) * 4,
        scratch_shapes=[
            vmem((T, 2 * HD), BF16),
            vmem((T, 2 * HD), BF16),
            vmem((T, 2 * HD), BF16),
            vmem((T, width), BF16),
            vmem((2 * HD, width), BF16),
            vmem((pairs, T), jnp.int32),
            vmem((1, 2 * pairs), jnp.int32),
            vmem((T, 2 * HD), BF16),
            vmem((2, T, HD), BF16),
            vmem((2, T, HD), BF16),
            vmem((nz, 2, 2, T, HD), BF16),
            vmem((ny, 2, 2, T, HD), BF16),
            vmem((pairs, T), F32),
            vmem((nz, B, T), F32),
            vmem((ny, B), F32),
            vmem((nz, ny, B, B), F32),
            vmem((nz, ny, B, B), F32),
            vmem((nz, ny, HD, B), F32),
            vmem((nz, ny, B), F32),
            vmem((nz, ny, B), F32),
            vmem((nz, ny, B), F32),
            vmem((ny, 3, ny, B), F32),
            vmem((nz, ny, B), F32),
            vmem((ny, ny, B), F32),
            vmem((ny, B), F32),
            vmem((ny, HD, B), BF16),
            vmem((ny, HD, B), BF16),
            vmem((2, ny, HD, B), BF16),
            vmem((ny, 2, T, cols), BF16),
            vmem((nz, zcols, 2 * HD), F32),
            vmem((nz, zcols, 2 * HD), F32),
            vmem((nz, B, HD), F32),
            vmem((nz, B, HD), F32),
            vmem((ny, HD, B), F32),
            vmem((2, half, 2, T, HD), BF16),
            vmem((2, half, 2, T, HD), BF16),
            vmem((2, half, 2, T, HD), F32),
            vmem((2, half, 2, T, HD), F32),
            vmem((ny, 2, HD, T), BF16),
            vmem((2, ny, HD, T), BF16),
            vmem((T, HD), F32),
            vmem((T, HD), F32),
            vmem((T, HD), BF16),
            vmem((T, HD), BF16),
            dma((7,)),
            dma((128,)),
            dma((nz, 2)),
            dma((ny, 2)),
            dma((2, ny)),
            dma((ny,)),
            dma((ny,)),
            dma((2, ny)),
            dma((nz,)),
            dma((2, 2, half, 2)),
            dma((2, ny)),
            dma((2,)),
        ],
        compiler_params=pltpu.CompilerParams(
            collective_id=0, has_side_effects=True, vmem_limit_bytes=63 * 1024 * 1024
        ),
    )(queries, keys, values, out_grad, w_out, frames_in, order_in)
    return results[:3] + (jnp.transpose(results[3]),)


def solution(mesh):
    ny, nz = {64: (4, 8), 32: (2, 8), 16: (2, 4)}[mesh.shape["ctx"]]
    placed = (
        P("ctx", "tp"),
        P("ctx", "tp"),
        P("ctx", "tp"),
        P("ctx", None),
        P("tp", None),
        P(),
        P(),
    )
    return jax.shard_map(
        functools.partial(shards, ny, nz),
        mesh=mesh,
        in_specs=placed,
        out_specs=(P("ctx", "tp"), P("ctx", "tp"), P("ctx", "tp"), P("tp", "ctx")),
        check_vma=False,
    )
```

```python
import functools
import math

import jax
import jax.numpy as jnp
from jax import lax
from jax.experimental import pallas as pl
from jax.experimental.pallas import tpu as pltpu
from jax.sharding import PartitionSpec as P

HD = 128
T = 128
B = 2 * T
MASKED = -1e30
FLOOR = -1e29
SCALE = HD**-0.5
EXP2_SCALE = SCALE * math.log2(math.e)
F32 = jnp.float32
BF16 = jnp.bfloat16
NT = (((1,), (1,)), ((), ()))
TN = (((0,), (0,)), ((), ()))
MESH = pl.DeviceIdType.MESH


def dot(a, b):
    return jnp.dot(a, b, preferred_element_type=F32)


def dot_general(a, b, dims):
    return lax.dot_general(a, b, dims, preferred_element_type=F32)


def kernel(
    ny,
    nz,
    q_hbm,
    k_hbm,
    v_hbm,
    og_hbm,
    w_hbm,
    fi_hbm,
    go_hbm,
    out_ref,
    gw_ref,
    q_in,
    k_in,
    v_in,
    og_in,
    w_in,
    fi_in,
    go_in,
    da,
    kv_other,
    qd_other,
    kv,
    qd,
    frames,
    kf,
    qf,
    wts,
    dps,
    v_t,
    mst,
    lst,
    dst,
    stats,
    cst,
    ysh,
    dlt,
    osend,
    orecv,
    att,
    ogb,
    gsend,
    grecv,
    acc_k,
    acc_v,
    acc_q,
    rsk_out,
    rsk_in,
    rsv_out,
    rsv_in,
    qsend,
    qrecv,
    finv_out,
    finv_in,
    fink_out,
    fink_in,
    in_sem,
    sent,
    z_r,
    y_r,
    og_r,
    st_r,
    o_r,
    att_r,
    g_r,
    rs_r,
    dq_r,
    fin_r,
):
    gq_ref, gk_ref, gv_ref = (out_ref.at[:, pl.ds(i * B, B)] for i in range(3))
    half = nz // 2
    me = lax.axis_index("ctx")
    x = me // (ny * nz)
    y = lax.rem(me // nz, ny)
    z = lax.rem(me, nz)
    px = 1 - x
    cols = og_in.shape[1] // (2 * ny)
    zcols = cols // nz

    def at(xx, yy, zz):
        return xx * (ny * nz) + yy * nz + zz

    partner = at(px, y, z)
    right = at(x, y, lax.rem(z + 1, nz))
    left = at(x, y, lax.rem(z + nz - 1, nz))
    ypos = [lax.rem(y + k, ny) for k in range(ny)]
    ypeer = [at(x, ypos[k], z) for k in range(ny)]
    ydiag = [at(px, ypos[k], z) for k in range(ny)]
    zpos = [lax.rem(z + k, nz) for k in range(nz)]
    zpeer = [at(x, y, zpos[k]) for k in range(nz)]
    zdiag = [at(px, y, zpos[k]) for k in range(nz)]

    started = []

    def send(src, dst_ref, r_sem, device):
        copy = pltpu.make_async_remote_copy(
            src_ref=src,
            dst_ref=dst_ref,
            send_sem=sent.at[len(started)],
            recv_sem=r_sem,
            device_id={"ctx": device},
            device_id_type=MESH,
        )
        copy.start()
        started.append(copy)

    def arrived(dst_ref, r_sem):
        pltpu.make_async_remote_copy(
            src_ref=dst_ref,
            dst_ref=dst_ref,
            send_sem=sent.at[0],
            recv_sem=r_sem,
            device_id={"ctx": partner},
            device_id_type=MESH,
        ).wait_recv()

    loads = [
        pltpu.make_async_copy(src, to, in_sem.at[i])
        for i, (src, to) in enumerate(
            [
                (k_hbm, k_in),
                (v_hbm, v_in),
                (w_hbm, w_in),
                (og_hbm, og_in),
                (q_hbm, q_in),
                (fi_hbm, fi_in),
                (go_hbm, go_in),
            ]
        )
    ]
    for load in loads:
        load.start()
    barrier = pltpu.get_barrier_semaphore()
    peers = ydiag + ypeer[1:] + zpeer[1:] + [zdiag[1], zdiag[nz - 1]]
    for peer in peers:
        pl.semaphore_signal(barrier, inc=1, device_id={"ctx": peer}, device_id_type=MESH)
    own_lanes = pl.ds(pl.multiple_of(x * HD, HD), HD)
    other_lanes = pl.ds(pl.multiple_of(px * HD, HD), HD)

    def stage(src, own, other, i):
        own[i] = src[:, own_lanes]
        other[i] = src[:, other_lanes]

    for load in loads:
        load.wait()
    stage(k_in, kv.at[0, 0], kv_other, 0)
    stage(v_in, kv.at[0, 0], kv_other, 1)
    da[...] = dot_general(og_in[...], w_in[...], NT).astype(BF16)
    stage(q_in, qd.at[y, 0], qd_other, 0)
    stage(da, qd.at[y, 0], qd_other, 1)

    go = go_in[...]
    fi = fi_in[...].astype(F32)
    pairs, lanes = fi.shape
    groups = go.shape[1]
    half_lanes = lanes // 2
    lane = lax.broadcasted_iota(jnp.int32, (pairs, lanes), 1)
    low = jnp.where(lane < half_lanes, fi, 0.0)
    high = jnp.where(lane >= half_lanes, fi, 0.0)
    low_up = jnp.concatenate([low[:, half_lanes:], low[:, :half_lanes]], axis=1)
    high_down = jnp.concatenate([high[:, half_lanes:], high[:, :half_lanes]], axis=1)
    row = lax.broadcasted_iota(jnp.int32, (pairs, groups), 0)
    holds = [(go == 2 * row + p).astype(F32).astype(BF16) for p in range(2)]
    group_id = lax.broadcasted_iota(jnp.int32, (groups, pairs), 0)
    pair_id = lax.broadcasted_iota(jnp.int32, (groups, pairs), 1)
    picks = [(group_id == 2 * pair_id + e).astype(F32).astype(BF16) for e in range(2)]
    total = jnp.zeros((pairs, lanes), F32)
    for p in range(2):
        for e in range(2):
            part = ((low, low_up), (high_down, high))[p][e]
            total += dot_general(dot(holds[p], picks[e]).astype(BF16), part.astype(BF16), TN)
    frames[...] = total
    across = jnp.transpose(total)
    device_lane = lax.broadcasted_iota(jnp.int32, (lanes, pairs), 1)
    distance = (
        [0] + [nz - s for s in range(1, half)] + [s for s in range(1, half)] + [half]
    )
    for slot in range(nz):
        for c in range(2):
            source = at(x if c == 0 else px, y, zpos[distance[slot]])
            column = jnp.sum(jnp.where(device_lane == source, across, 0.0), axis=1, keepdims=True)
            kf[slot, pl.ds(c * T, T), :] = jnp.broadcast_to(column, (T, lanes))
    for b in range(ny):
        qf[pl.ds(b, 1), pl.ds(0, T)] = frames[pl.ds(at(x, b, z), 1), :]
        qf[pl.ds(b, 1), pl.ds(T, T)] = frames[pl.ds(at(px, b, z), 1), :]

    pl.semaphore_wait(barrier, len(peers))

    def left_slot(s):
        return s if s < half else nz - 1

    def right_slot(s):
        return half - 1 + s if s < half else nz - 1

    def z_send(way, s, c):
        slots = (left_slot, right_slot)[way]
        k = 1 if way == 0 else nz - 1
        slot = slots(s)
        if s > 1:
            send(kv.at[slots(s - 1), c], kv.at[slot, c], z_r.at[slot, c], zpeer[k])
        elif c == 0:
            send(kv.at[0, 0], kv.at[slot, 0], z_r.at[slot, 0], zpeer[k])
        else:
            send(kv_other, kv.at[slot, 1], z_r.at[slot, 1], zdiag[k])

    def z_arrived(slot, c):
        arrived(kv.at[slot, c], z_r.at[slot, c])

    def relay(s):
        for c in range(2):
            for way in range(2):
                z_arrived((left_slot, right_slot)[way](s), c)
                if s + 1 < half or way == c:
                    z_send(way, s + 1, c)

    for c in range(2):
        for way in range(2):
            z_send(way, 1, c)
    for k in range(1, ny):
        send(qd.at[y, 0], qd.at[y, 0], y_r.at[ny - k, 0], ypeer[k])
    for k in range(ny):
        send(qd_other, qd.at[y, 1], y_r.at[(ny - k) % ny, 1], ydiag[k])
    send(kv_other, kv.at[0, 1], z_r.at[0, 1], partner)

    def og_lanes(xx, yy):
        return pl.ds(pl.multiple_of((xx * ny + yy) * cols, cols), cols)

    og_targets = [(x, k, ypeer[k]) for k in range(1, ny)] + [(px, k, ydiag[k]) for k in range(ny)]

    def og_send():
        ogb[y, x] = og_in[:, og_lanes(x, y)]
        for i, (xx, k, device) in enumerate(og_targets):
            side = 0 if i < ny - 1 else 1
            r = (ny - k) % ny
            send(
                og_in.at[:, og_lanes(xx, ypos[k])],
                ogb.at[y, x],
                og_r.at[side, r],
                device,
            )

    def forward(slot):
        kb = kv[slot, :, 0].reshape(B, HD)
        vb = kv[slot, :, 1].reshape(B, HD)
        v_t[slot] = jnp.transpose(vb)
        key_frames = jnp.concatenate([kf[slot], kf[slot]], axis=1)

        def body(b, carry):
            scores = dot_general(kb, qd[b, :, 0].reshape(B, HD), NT)
            grads = dot_general(vb, qd[b, :, 1].reshape(B, HD), NT)
            scores = jnp.where(key_frames <= qf[pl.ds(b, 1), :], scores, MASKED)
            top = jnp.maximum(jnp.max(scores, axis=0, keepdims=True), FLOOR)
            weights = jnp.exp2((scores - top) * EXP2_SCALE)
            wts[slot, b] = weights
            dps[slot, b] = grads
            mst[slot, pl.ds(b, 1), :] = top
            lst[slot, pl.ds(b, 1), :] = jnp.sum(weights, axis=0, keepdims=True)
            dst[slot, pl.ds(b, 1), :] = jnp.sum(weights * grads, axis=0, keepdims=True)
            return carry

        lax.fori_loop(0, ny, body, 0, unroll=True)

    for s in range(1, max(half - 1, 2)):
        relay(s)
    z_arrived(0, 1)
    for k in range(ny):
        for c in range(2):
            if k + c > 0:
                arrived(qd.at[ypos[k], c], y_r.at[k, c])
    og_send()
    forward(0)
    for s in range(1, half):
        if s > 1 and s == half - 1:
            relay(s)
        forward(left_slot(s))
        forward(right_slot(s))
    z_arrived(nz - 1, 0)
    z_arrived(nz - 1, 1)
    forward(nz - 1)

    tops = mst[...]
    own_top = jnp.max(tops, axis=0)
    shares = jnp.exp2((tops - own_top[None]) * EXP2_SCALE)
    stats[y, 0] = own_top
    stats[y, 1] = jnp.sum(shares * lst[...], axis=0)
    stats[y, 2] = jnp.sum(shares * dst[...], axis=0)
    for k in range(1, ny):
        send(stats.at[y], stats.at[y], st_r.at[ny - k], ypeer[k])

    cst[...] = shares

    for k in [*range(1, ny), 0]:
        b = ypos[k]
        part = jnp.zeros((HD, B), F32)
        for slot in range(nz):
            part += dot(v_t[slot], (wts[slot, b] * cst[slot, pl.ds(b, 1), :]).astype(BF16))
        osend[b] = part.astype(BF16)
        if k > 0:
            send(osend.at[b], orecv.at[ny - k], o_r.at[ny - k], ypeer[k])

    for k in range(1, ny):
        arrived(stats.at[ypos[k]], st_r.at[k])
    all_top = stats[0, 0]
    for b in range(1, ny):
        all_top = jnp.maximum(all_top, stats[b, 0])
    row_total = jnp.zeros_like(all_top)
    delta = jnp.zeros_like(all_top)
    for b in range(ny):
        share = jnp.exp2((stats[b, 0] - all_top) * EXP2_SCALE)
        row_total += share * stats[b, 1]
        delta += share * stats[b, 2]
        ysh[b] = share
    inverse = 1.0 / row_total
    for b in range(ny):
        ysh[b] = ysh[b] * inverse
    dlt[...] = delta * inverse
    cst[...] = jnp.exp2((tops - all_top[None]) * EXP2_SCALE) * inverse[None]

    acc_q[...] = jnp.zeros_like(acc_q)

    def backward(slot):
        k_t = jnp.transpose(kv[slot, :, 0].reshape(B, HD))
        acc_k[slot] = jnp.zeros((B, HD), F32)
        acc_v[slot] = jnp.zeros((B, HD), F32)

        def body(b, carry):
            probs = wts[slot, b] * cst[slot, pl.ds(b, 1), :]
            grad_scores = (probs * (dps[slot, b] - dlt[pl.ds(b, 1), :])).astype(BF16)
            acc_v[slot] += dot(probs.astype(BF16), qd[b, :, 1].reshape(B, HD))
            acc_k[slot] += dot(grad_scores, qd[b, :, 0].reshape(B, HD))
            acc_q[b] += dot(k_t, grad_scores)
            return carry

        lax.fori_loop(0, ny, body, 0, unroll=True)

    pieces = (
        (0, T // 2, acc_v, rsv_out, rsv_in),
        (T // 2, T // 2, acc_v, rsv_out, rsv_in),
        (0, T, acc_k, rsk_out, rsk_in),
    )

    def reduce_send(way, step, c, t, arrival):
        d = half + 1 - step
        i = step - 1
        slot = (right_slot, left_slot)[way](d)
        k = 1 if way == 0 else nz - 1
        device = zdiag[k] if step == half and c == 1 else zpeer[k]
        first, count, acc, src, to = pieces[t]
        rows = pl.ds(first, count)
        part = acc[slot, pl.ds(c * T + first, count), :]
        if arrival:
            arrived(to.at[way, i - 1, c, rows], rs_r.at[t, way, i - 1, c])
            part += to[way, i - 1, c, rows].astype(F32)
        src[way, i, c, rows] = part.astype(src.dtype)
        send(src.at[way, i, c, rows], to.at[way, i, c, rows], rs_r.at[t, way, i, c], device)

    def reduce_chunk(way, step, c):
        for t in range(3):
            reduce_send(way, step, c, t, False)

    def reduce_rest(step):
        for turn in range(2 if step > 2 else 1):
            for t in range(3):
                for way in range(2):
                    last = turn == 1 or step == 2
                    reduce_send(way, step, way if last else 1 - way, t, True)

    def attended_rows():
        for k in range(1, ny):
            arrived(orecv.at[k], o_r.at[k])
        rows_att = osend[y].astype(F32) * ysh[y, pl.ds(y, 1), :]
        for k in range(1, ny):
            rows_att += orecv[k].astype(F32) * ysh[ypos[k], pl.ds(y, 1), :]
        att[x, y] = rows_att.astype(BF16)
        for i, (xx, k, device) in enumerate(og_targets):
            side = 0 if i < ny - 1 else 1
            send(att.at[x, y], att.at[x, y], att_r.at[side, (ny - k) % ny], device)

    def query_part():
        backward(0)
        for t, (acc, src, to) in enumerate(((acc_v, finv_out, finv_in), (acc_k, fink_out, fink_in))):
            src[...] = acc[0, pl.ds(T, T), :].astype(src.dtype)
            send(src, to, fin_r.at[t], partner)
        for b in range(ny):
            for c in range(2):
                qsend[b, c] = acc_q[b, :, pl.ds(c * T, T)].astype(BF16)
        for k in range(ny):
            r = (ny - k) % ny
            if k > 0:
                send(qsend.at[ypos[k], 0], qrecv.at[0, r], dq_r.at[0, r], ypeer[k])
            send(qsend.at[ypos[k], 1], qrecv.at[1, r], dq_r.at[1, r], ydiag[k])

    def weight_part():
        for i, (xx, k, device) in enumerate(og_targets):
            side = 0 if i < ny - 1 else 1
            source_x = x if side == 0 else px
            arrived(ogb.at[ypos[k], source_x], og_r.at[side, k])
            arrived(att.at[source_x, ypos[k]], att_r.at[side, k])
        for h in range(2):
            part = jnp.zeros((HD, cols), F32)
            for b in range(ny):
                for c in range(2):
                    part += dot(att[h, b, :, pl.ds(c * T, T)], ogb[b, h ^ c])
            gsend[:, :, pl.ds(h * HD, HD)] = jnp.transpose(part).reshape(nz, zcols, HD)
        for k in range(1, nz):
            send(gsend.at[zpos[k]], grecv.at[nz - k], g_r.at[nz - k], zpeer[k])

    backward(nz - 1)
    reduce_chunk(0, 1, 0)
    reduce_chunk(1, 1, 1)
    backward(right_slot(half - 1))
    reduce_chunk(0, 2, 1)
    backward(left_slot(half - 1))
    reduce_chunk(1, 2, 0)
    attended_rows()
    for d in range(half - 2, 0, -1):
        backward(right_slot(d))
        backward(left_slot(d))
    query_part()
    for step in range(2, half + 1):
        if step == max(half, 3):
            weight_part()
        reduce_rest(step)
    if half == 2:
        weight_part()

    for t, (acc, src, to) in enumerate(((acc_v, finv_out, finv_in), (acc_k, fink_out, fink_in))):
        arrived(to, fin_r.at[t])
    for k in range(ny):
        for c in range(2):
            if k + c > 0:
                arrived(qrecv.at[c, k], dq_r.at[c, k])
    for c, lanes_out in enumerate((own_lanes, other_lanes)):
        rows_q = qsend[y, 0].astype(F32) if c == 0 else qrecv[1, 0].astype(F32)
        for k in range(1, ny):
            rows_q += qrecv[c, k].astype(F32)
        gq_ref[:, lanes_out] = jnp.transpose(rows_q * SCALE).astype(BF16)
    for c, lanes_out in ((1, other_lanes), (0, own_lanes)):
        part_v = finv_in[...] if c == 1 else acc_v[0, pl.ds(0, T), :]
        part_k = fink_in[...].astype(F32) if c == 1 else acc_k[0, pl.ds(0, T), :]
        for way in (0, 1) if c == 1 else (1, 0):
            for t, (first, count, acc, src, to) in enumerate(pieces):
                arrived(to.at[way, half - 1, c, pl.ds(first, count)], rs_r.at[t, way, half - 1, c])
            part_v += rsv_in[way, half - 1, c]
            part_k += rsk_in[way, half - 1, c].astype(F32)
        gv_ref[:, lanes_out] = part_v.astype(BF16)
        gk_ref[:, lanes_out] = (part_k * SCALE).astype(BF16)

    for k in range(1, nz):
        arrived(grecv.at[k], g_r.at[k])
    weight_rows = gsend[z]
    for k in range(1, nz):
        weight_rows += grecv[k]
    gw_ref[...] = weight_rows

    for copy in started:
        copy.wait_send()


def shards(ny, nz, queries, keys, values, out_grad, w_out, frame_index, group_order):
    half = nz // 2
    width = out_grad.shape[1]
    cols = width // (2 * ny)
    zcols = cols // nz
    pairs = group_order.shape[0] // 2
    frames_in = frame_index.reshape(pairs, T)
    order_in = group_order.reshape(1, 2 * pairs)
    vmem = pltpu.VMEM
    dma = pltpu.SemaphoreType.DMA
    any_spec = pl.BlockSpec(memory_space=pltpu.HBM)
    out_spec = pl.BlockSpec(memory_space=pltpu.VMEM)
    results = pl.pallas_call(
        functools.partial(kernel, ny, nz),
        out_shape=(
            jax.ShapeDtypeStruct((T, 6 * HD), BF16),
            jax.ShapeDtypeStruct((zcols, 2 * HD), F32),
        ),
        in_specs=[any_spec] * 7,
        out_specs=(out_spec,) * 2,
        scratch_shapes=[
            vmem((T, 2 * HD), BF16),
            vmem((T, 2 * HD), BF16),
            vmem((T, 2 * HD), BF16),
            vmem((T, width), BF16),
            vmem((2 * HD, width), BF16),
            vmem((pairs, T), jnp.int32),
            vmem((1, 2 * pairs), jnp.int32),
            vmem((T, 2 * HD), BF16),
            vmem((2, T, HD), BF16),
            vmem((2, T, HD), BF16),
            vmem((nz, 2, 2, T, HD), BF16),
            vmem((ny, 2, 2, T, HD), BF16),
            vmem((pairs, T), F32),
            vmem((nz, B, T), F32),
            vmem((ny, B), F32),
            vmem((nz, ny, B, B), F32),
            vmem((nz, ny, B, B), F32),
            vmem((nz, HD, B), BF16),
            vmem((nz, ny, B), F32),
            vmem((nz, ny, B), F32),
            vmem((nz, ny, B), F32),
            vmem((ny, 3, ny, B), F32),
            vmem((nz, ny, B), F32),
            vmem((ny, ny, B), F32),
            vmem((ny, B), F32),
            vmem((ny, HD, B), BF16),
            vmem((ny, HD, B), BF16),
            vmem((2, ny, HD, B), BF16),
            vmem((ny, 2, T, cols), BF16),
            vmem((nz, zcols, 2 * HD), F32),
            vmem((nz, zcols, 2 * HD), F32),
            vmem((nz, B, HD), F32),
            vmem((nz, B, HD), F32),
            vmem((ny, HD, B), F32),
            vmem((2, half, 2, T, HD), BF16),
            vmem((2, half, 2, T, HD), BF16),
            vmem((2, half, 2, T, HD), F32),
            vmem((2, half, 2, T, HD), F32),
            vmem((ny, 2, HD, T), BF16),
            vmem((2, ny, HD, T), BF16),
            vmem((T, HD), F32),
            vmem((T, HD), F32),
            vmem((T, HD), BF16),
            vmem((T, HD), BF16),
            dma((7,)),
            dma((160,)),
            dma((nz, 2)),
            dma((ny, 2)),
            dma((2, ny)),
            dma((ny,)),
            dma((ny,)),
            dma((2, ny)),
            dma((nz,)),
            dma((3, 2, half, 2)),
            dma((2, ny)),
            dma((2,)),
        ],
        compiler_params=pltpu.CompilerParams(
            collective_id=0, has_side_effects=True, vmem_limit_bytes=63 * 1024 * 1024
        ),
    )(queries, keys, values, out_grad, w_out, frames_in, order_in)
    o, g = results
    return o[:, :B], o[:, B:2*B], o[:, 2*B:], jnp.transpose(g)


def solution(mesh):
    ny, nz = {64: (4, 8), 32: (2, 8), 16: (2, 4)}[mesh.shape["ctx"]]
    placed = (
        P("ctx", "tp"),
        P("ctx", "tp"),
        P("ctx", "tp"),
        P("ctx", None),
        P("tp", None),
        P(),
        P(),
    )
    return jax.shard_map(
        functools.partial(shards, ny, nz),
        mesh=mesh,
        in_specs=placed,
        out_specs=(P("ctx", "tp"), P("ctx", "tp"), P("ctx", "tp"), P("tp", "ctx")),
        check_vma=False,
    )
```

```python
import functools
import math

import jax
import jax.numpy as jnp
from jax import lax
from jax.experimental import pallas as pl
from jax.experimental.pallas import tpu as pltpu
from jax.sharding import PartitionSpec as P

HD = 128
T = 128
B = 2 * T
MASKED = -1e30
FLOOR = -1e29
SCALE = HD**-0.5
EXP2_SCALE = SCALE * math.log2(math.e)
F32 = jnp.float32
BF16 = jnp.bfloat16
NT = (((1,), (1,)), ((), ()))
TN = (((0,), (0,)), ((), ()))
MESH = pl.DeviceIdType.MESH


def dot(a, b):
    return jnp.dot(a, b, preferred_element_type=F32)


def dot_general(a, b, dims):
    return lax.dot_general(a, b, dims, preferred_element_type=F32)


def kernel(
    ny,
    nz,
    q_hbm,
    k_hbm,
    v_hbm,
    og_hbm,
    w_hbm,
    fi_hbm,
    go_hbm,
    out_ref,
    gw_ref,
    q_in,
    k_in,
    v_in,
    og_in,
    w_in,
    fi_in,
    go_in,
    da,
    kv_other,
    qd_other,
    kv,
    qd,
    frames,
    kf,
    qf,
    wts,
    dps,
    v_t,
    mst,
    lst,
    dst,
    stats,
    cst,
    ysh,
    dlt,
    osend,
    orecv,
    att,
    ogb,
    gsend,
    grecv,
    acc_k,
    acc_v,
    acc_q,
    rsk_out,
    rsk_in,
    rsv_out,
    rsv_in,
    qsend,
    qrecv,
    finv_out,
    finv_in,
    fink_out,
    fink_in,
    in_sem,
    sent,
    z_r,
    y_r,
    og_r,
    st_r,
    o_r,
    att_r,
    g_r,
    rs_r,
    dq_r,
    fin_r,
):
    gq_ref, gk_ref, gv_ref = (out_ref.at[:, pl.ds(i * B, B)] for i in range(3))
    half = nz // 2
    me = lax.axis_index("ctx")
    x = me // (ny * nz)
    y = lax.rem(me // nz, ny)
    z = lax.rem(me, nz)
    px = 1 - x
    cols = og_in.shape[1] // (2 * ny)
    zcols = cols // nz

    def at(xx, yy, zz):
        return xx * (ny * nz) + yy * nz + zz

    partner = at(px, y, z)
    right = at(x, y, lax.rem(z + 1, nz))
    left = at(x, y, lax.rem(z + nz - 1, nz))
    ypos = [lax.rem(y + k, ny) for k in range(ny)]
    ypeer = [at(x, ypos[k], z) for k in range(ny)]
    ydiag = [at(px, ypos[k], z) for k in range(ny)]
    zpos = [lax.rem(z + k, nz) for k in range(nz)]
    zpeer = [at(x, y, zpos[k]) for k in range(nz)]
    zdiag = [at(px, y, zpos[k]) for k in range(nz)]

    started = []

    def send(src, dst_ref, r_sem, device):
        copy = pltpu.make_async_remote_copy(
            src_ref=src,
            dst_ref=dst_ref,
            send_sem=sent.at[len(started)],
            recv_sem=r_sem,
            device_id={"ctx": device},
            device_id_type=MESH,
        )
        copy.start()
        started.append(copy)

    def arrived(dst_ref, r_sem):
        pltpu.make_async_remote_copy(
            src_ref=dst_ref,
            dst_ref=dst_ref,
            send_sem=sent.at[0],
            recv_sem=r_sem,
            device_id={"ctx": partner},
            device_id_type=MESH,
        ).wait_recv()

    loads = [
        pltpu.make_async_copy(src, to, in_sem.at[i])
        for i, (src, to) in enumerate(
            [
                (k_hbm, k_in),
                (v_hbm, v_in),
                (w_hbm, w_in),
                (og_hbm, og_in),
                (q_hbm, q_in),
                (fi_hbm, fi_in),
                (go_hbm, go_in),
            ]
        )
    ]
    for load in loads:
        load.start()
    barrier = pltpu.get_barrier_semaphore()
    peers = ydiag + ypeer[1:] + zpeer[1:] + [zdiag[1], zdiag[nz - 1]]
    for peer in peers:
        pl.semaphore_signal(barrier, inc=1, device_id={"ctx": peer}, device_id_type=MESH)
    own_lanes = pl.ds(pl.multiple_of(x * HD, HD), HD)
    other_lanes = pl.ds(pl.multiple_of(px * HD, HD), HD)

    def stage(src, own, other, i):
        own[i] = src[:, own_lanes]
        other[i] = src[:, other_lanes]

    for load in loads:
        load.wait()
    stage(k_in, kv.at[0, 0], kv_other, 0)
    stage(v_in, kv.at[0, 0], kv_other, 1)
    da[...] = dot_general(og_in[...], w_in[...], NT).astype(BF16)
    stage(q_in, qd.at[y, 0], qd_other, 0)
    stage(da, qd.at[y, 0], qd_other, 1)

    go = go_in[...]
    fi = fi_in[...].astype(F32)
    pairs, lanes = fi.shape
    groups = go.shape[1]
    half_lanes = lanes // 2
    lane = lax.broadcasted_iota(jnp.int32, (pairs, lanes), 1)
    low = jnp.where(lane < half_lanes, fi, 0.0)
    high = jnp.where(lane >= half_lanes, fi, 0.0)
    low_up = jnp.concatenate([low[:, half_lanes:], low[:, :half_lanes]], axis=1)
    high_down = jnp.concatenate([high[:, half_lanes:], high[:, :half_lanes]], axis=1)
    row = lax.broadcasted_iota(jnp.int32, (pairs, groups), 0)
    holds = [(go == 2 * row + p).astype(F32).astype(BF16) for p in range(2)]
    group_id = lax.broadcasted_iota(jnp.int32, (groups, pairs), 0)
    pair_id = lax.broadcasted_iota(jnp.int32, (groups, pairs), 1)
    picks = [(group_id == 2 * pair_id + e).astype(F32).astype(BF16) for e in range(2)]
    total = jnp.zeros((pairs, lanes), F32)
    for p in range(2):
        for e in range(2):
            part = ((low, low_up), (high_down, high))[p][e]
            total += dot_general(dot(holds[p], picks[e]).astype(BF16), part.astype(BF16), TN)
    frames[...] = total
    across = jnp.transpose(total)
    device_lane = lax.broadcasted_iota(jnp.int32, (lanes, pairs), 1)
    distance = (
        [0] + [nz - s for s in range(1, half)] + [s for s in range(1, half)] + [half]
    )
    for slot in range(nz):
        for c in range(2):
            source = at(x if c == 0 else px, y, zpos[distance[slot]])
            column = jnp.sum(jnp.where(device_lane == source, across, 0.0), axis=1, keepdims=True)
            kf[slot, pl.ds(c * T, T), :] = jnp.broadcast_to(column, (T, lanes))
    for b in range(ny):
        qf[pl.ds(b, 1), pl.ds(0, T)] = frames[pl.ds(at(x, b, z), 1), :]
        qf[pl.ds(b, 1), pl.ds(T, T)] = frames[pl.ds(at(px, b, z), 1), :]

    pl.semaphore_wait(barrier, len(peers))

    def left_slot(s):
        return s if s < half else nz - 1

    def right_slot(s):
        return half - 1 + s if s < half else nz - 1

    def z_send(way, s, c):
        slots = (left_slot, right_slot)[way]
        k = 1 if way == 0 else nz - 1
        slot = slots(s)
        if s > 1:
            send(kv.at[slots(s - 1), c], kv.at[slot, c], z_r.at[slot, c], zpeer[k])
        elif c == 0:
            send(kv.at[0, 0], kv.at[slot, 0], z_r.at[slot, 0], zpeer[k])
        else:
            send(kv_other, kv.at[slot, 1], z_r.at[slot, 1], zdiag[k])

    def z_arrived(slot, c):
        arrived(kv.at[slot, c], z_r.at[slot, c])

    def z_send_far(way, source, peers_far):
        k = 2 if way == 0 else nz - 2
        send(source, kv.at[nz - 1, way], z_r.at[nz - 1, way], peers_far[k])

    def relay(s):
        for c in range(2):
            for way in range(2):
                slot = (left_slot, right_slot)[way](s)
                z_arrived(slot, c)
                if s + 1 < half:
                    z_send(way, s + 1, c)
                if s == half - 2 and way == c:
                    z_send_far(way, kv.at[slot, c], zpeer)

    for c in range(2):
        for way in range(2):
            z_send(way, 1, c)
    if half == 2:
        z_send_far(0, kv.at[0, 0], zpeer)
        z_send_far(1, kv_other, zdiag)
    for k in range(1, ny):
        send(qd.at[y, 0], qd.at[y, 0], y_r.at[ny - k, 0], ypeer[k])
    for k in range(ny):
        send(qd_other, qd.at[y, 1], y_r.at[(ny - k) % ny, 1], ydiag[k])
    send(kv_other, kv.at[0, 1], z_r.at[0, 1], partner)

    def og_lanes(xx, yy):
        return pl.ds(pl.multiple_of((xx * ny + yy) * cols, cols), cols)

    og_targets = [(x, k, ypeer[k]) for k in range(1, ny)] + [(px, k, ydiag[k]) for k in range(ny)]

    def og_send():
        ogb[y, x] = og_in[:, og_lanes(x, y)]
        for i, (xx, k, device) in enumerate(og_targets):
            side = 0 if i < ny - 1 else 1
            r = (ny - k) % ny
            send(
                og_in.at[:, og_lanes(xx, ypos[k])],
                ogb.at[y, x],
                og_r.at[side, r],
                device,
            )

    def forward(slot):
        kb = kv[slot, :, 0].reshape(B, HD)
        vb = kv[slot, :, 1].reshape(B, HD)
        v_t[slot] = jnp.transpose(vb)
        key_frames = jnp.concatenate([kf[slot], kf[slot]], axis=1)

        def body(b, carry):
            scores = dot_general(kb, qd[b, :, 0].reshape(B, HD), NT)
            grads = dot_general(vb, qd[b, :, 1].reshape(B, HD), NT)
            scores = jnp.where(key_frames <= qf[pl.ds(b, 1), :], scores, MASKED)
            top = jnp.maximum(jnp.max(scores, axis=0, keepdims=True), FLOOR)
            weights = jnp.exp2((scores - top) * EXP2_SCALE)
            wts[slot, b] = weights
            dps[slot, b] = grads
            mst[slot, pl.ds(b, 1), :] = top
            lst[slot, pl.ds(b, 1), :] = jnp.sum(weights, axis=0, keepdims=True)
            dst[slot, pl.ds(b, 1), :] = jnp.sum(weights * grads, axis=0, keepdims=True)
            return carry

        lax.fori_loop(0, ny, body, 0, unroll=True)

    for s in range(1, max(half - 1, 2)):
        relay(s)
    z_arrived(0, 1)
    for k in range(ny):
        for c in range(2):
            if k + c > 0:
                arrived(qd.at[ypos[k], c], y_r.at[k, c])
    og_send()
    forward(0)
    for s in range(1, half):
        if s > 1 and s == half - 1:
            relay(s)
        forward(left_slot(s))
        forward(right_slot(s))
    z_arrived(nz - 1, 0)
    z_arrived(nz - 1, 1)
    forward(nz - 1)

    tops = mst[...]
    own_top = jnp.max(tops, axis=0)
    shares = jnp.exp2((tops - own_top[None]) * EXP2_SCALE)
    stats[y, 0] = own_top
    stats[y, 1] = jnp.sum(shares * lst[...], axis=0)
    stats[y, 2] = jnp.sum(shares * dst[...], axis=0)
    for k in range(1, ny):
        send(stats.at[y], stats.at[y], st_r.at[ny - k], ypeer[k])

    cst[...] = shares

    for k in [*range(1, ny), 0]:
        b = ypos[k]
        part = jnp.zeros((HD, B), F32)
        for slot in range(nz):
            part += dot(v_t[slot], (wts[slot, b] * cst[slot, pl.ds(b, 1), :]).astype(BF16))
        osend[b] = part.astype(BF16)
        if k > 0:
            send(osend.at[b], orecv.at[ny - k], o_r.at[ny - k], ypeer[k])

    for k in range(1, ny):
        arrived(stats.at[ypos[k]], st_r.at[k])
    all_top = stats[0, 0]
    for b in range(1, ny):
        all_top = jnp.maximum(all_top, stats[b, 0])
    row_total = jnp.zeros_like(all_top)
    delta = jnp.zeros_like(all_top)
    for b in range(ny):
        share = jnp.exp2((stats[b, 0] - all_top) * EXP2_SCALE)
        row_total += share * stats[b, 1]
        delta += share * stats[b, 2]
        ysh[b] = share
    inverse = 1.0 / row_total
    for b in range(ny):
        ysh[b] = ysh[b] * inverse
    dlt[...] = delta * inverse
    cst[...] = jnp.exp2((tops - all_top[None]) * EXP2_SCALE) * inverse[None]

    acc_q[...] = jnp.zeros_like(acc_q)

    def backward(slot):
        k_t = jnp.transpose(kv[slot, :, 0].reshape(B, HD))
        acc_k[slot] = jnp.zeros((B, HD), F32)
        acc_v[slot] = jnp.zeros((B, HD), F32)

        def body(b, carry):
            probs = wts[slot, b] * cst[slot, pl.ds(b, 1), :]
            grad_scores = (probs * (dps[slot, b] - dlt[pl.ds(b, 1), :])).astype(BF16)
            acc_v[slot] += dot(probs.astype(BF16), qd[b, :, 1].reshape(B, HD))
            acc_k[slot] += dot(grad_scores, qd[b, :, 0].reshape(B, HD))
            acc_q[b] += dot(k_t, grad_scores)
            return carry

        lax.fori_loop(0, ny, body, 0, unroll=True)

    pieces = (
        (0, T, acc_v, rsv_out, rsv_in),
        (0, T, acc_k, rsk_out, rsk_in),
    )

    def reduce_send(way, step, c, t, arrival):
        d = half + 1 - step
        i = step - 1
        slot = (right_slot, left_slot)[way](d)
        k = 1 if way == 0 else nz - 1
        device = zdiag[k] if step == half and c == 1 else zpeer[k]
        first, count, acc, src, to = pieces[t]
        rows = pl.ds(first, count)
        part = acc[slot, pl.ds(c * T + first, count), :]
        if arrival:
            arrived(to.at[way, i - 1, c, rows], rs_r.at[t, way, i - 1, c])
            part += to[way, i - 1, c, rows].astype(F32)
        src[way, i, c, rows] = part.astype(src.dtype)
        send(src.at[way, i, c, rows], to.at[way, i, c, rows], rs_r.at[t, way, i, c], device)

    def reduce_chunk(way, step, c):
        for t in range(2):
            reduce_send(way, step, c, t, False)

    def reduce_rest(step):
        for turn in range(2 if step > 2 else 1):
            for t in range(2):
                for way in range(2):
                    last = turn == 1 or step == 2
                    reduce_send(way, step, way if last else 1 - way, t, True)

    def attended_rows():
        for k in range(1, ny):
            arrived(orecv.at[k], o_r.at[k])
        rows_att = osend[y].astype(F32) * ysh[y, pl.ds(y, 1), :]
        for k in range(1, ny):
            rows_att += orecv[k].astype(F32) * ysh[ypos[k], pl.ds(y, 1), :]
        att[x, y] = rows_att.astype(BF16)
        for i, (xx, k, device) in enumerate(og_targets):
            side = 0 if i < ny - 1 else 1
            send(att.at[x, y], att.at[x, y], att_r.at[side, (ny - k) % ny], device)

    def query_part():
        backward(0)
        for t, (acc, src, to) in enumerate(((acc_v, finv_out, finv_in), (acc_k, fink_out, fink_in))):
            src[...] = acc[0, pl.ds(T, T), :].astype(src.dtype)
            send(src, to, fin_r.at[t], partner)
        for b in range(ny):
            for c in range(2):
                qsend[b, c] = acc_q[b, :, pl.ds(c * T, T)].astype(BF16)
        for k in range(ny):
            r = (ny - k) % ny
            if k > 0:
                send(qsend.at[ypos[k], 0], qrecv.at[0, r], dq_r.at[0, r], ypeer[k])
            send(qsend.at[ypos[k], 1], qrecv.at[1, r], dq_r.at[1, r], ydiag[k])

    def weight_part():
        for i, (xx, k, device) in enumerate(og_targets):
            side = 0 if i < ny - 1 else 1
            source_x = x if side == 0 else px
            arrived(ogb.at[ypos[k], source_x], og_r.at[side, k])
            arrived(att.at[source_x, ypos[k]], att_r.at[side, k])
        for h in range(2):
            part = jnp.zeros((HD, cols), F32)
            for b in range(ny):
                for c in range(2):
                    part += dot(att[h, b, :, pl.ds(c * T, T)], ogb[b, h ^ c])
            gsend[:, :, pl.ds(h * HD, HD)] = jnp.transpose(part).reshape(nz, zcols, HD)
        for k in range(1, nz):
            send(gsend.at[zpos[k]], grecv.at[nz - k], g_r.at[nz - k], zpeer[k])

    backward(nz - 1)
    reduce_chunk(0, 1, 0)
    reduce_chunk(1, 1, 1)
    backward(right_slot(half - 1))
    reduce_chunk(0, 2, 1)
    backward(left_slot(half - 1))
    reduce_chunk(1, 2, 0)
    attended_rows()
    for d in range(half - 2, 0, -1):
        backward(right_slot(d))
        backward(left_slot(d))
    query_part()
    for step in range(2, half + 1):
        if step == max(half, 3):
            weight_part()
        reduce_rest(step)
    if half == 2:
        weight_part()

    for t, (acc, src, to) in enumerate(((acc_v, finv_out, finv_in), (acc_k, fink_out, fink_in))):
        arrived(to, fin_r.at[t])
    for k in range(ny):
        for c in range(2):
            if k + c > 0:
                arrived(qrecv.at[c, k], dq_r.at[c, k])
    for c, lanes_out in enumerate((own_lanes, other_lanes)):
        rows_q = qsend[y, 0].astype(F32) if c == 0 else qrecv[1, 0].astype(F32)
        for k in range(1, ny):
            rows_q += qrecv[c, k].astype(F32)
        gq_ref[:, lanes_out] = jnp.transpose(rows_q * SCALE).astype(BF16)
    for c, lanes_out in ((1, other_lanes), (0, own_lanes)):
        part_v = finv_in[...] if c == 1 else acc_v[0, pl.ds(0, T), :]
        part_k = fink_in[...].astype(F32) if c == 1 else acc_k[0, pl.ds(0, T), :]
        for way in (0, 1) if c == 1 else (1, 0):
            for t, (first, count, acc, src, to) in enumerate(pieces):
                arrived(to.at[way, half - 1, c, pl.ds(first, count)], rs_r.at[t, way, half - 1, c])
            part_v += rsv_in[way, half - 1, c]
            part_k += rsk_in[way, half - 1, c].astype(F32)
        gv_ref[:, lanes_out] = part_v.astype(BF16)
        gk_ref[:, lanes_out] = (part_k * SCALE).astype(BF16)

    for k in range(1, nz):
        arrived(grecv.at[k], g_r.at[k])
    weight_rows = gsend[z]
    for k in range(1, nz):
        weight_rows += grecv[k]
    gw_ref[...] = weight_rows

    for copy in started:
        copy.wait_send()


def shards(ny, nz, queries, keys, values, out_grad, w_out, frame_index, group_order):
    half = nz // 2
    width = out_grad.shape[1]
    cols = width // (2 * ny)
    zcols = cols // nz
    pairs = group_order.shape[0] // 2
    frames_in = frame_index.reshape(pairs, T)
    order_in = group_order.reshape(1, 2 * pairs)
    vmem = pltpu.VMEM
    dma = pltpu.SemaphoreType.DMA
    any_spec = pl.BlockSpec(memory_space=pltpu.HBM)
    out_spec = pl.BlockSpec(memory_space=pltpu.VMEM)
    results = pl.pallas_call(
        functools.partial(kernel, ny, nz),
        out_shape=(
            jax.ShapeDtypeStruct((T, 6 * HD), BF16),
            jax.ShapeDtypeStruct((zcols, 2 * HD), F32),
        ),
        in_specs=[any_spec] * 7,
        out_specs=(out_spec,) * 2,
        scratch_shapes=[
            vmem((T, 2 * HD), BF16),
            vmem((T, 2 * HD), BF16),
            vmem((T, 2 * HD), BF16),
            vmem((T, width), BF16),
            vmem((2 * HD, width), BF16),
            vmem((pairs, T), jnp.int32),
            vmem((1, 2 * pairs), jnp.int32),
            vmem((T, 2 * HD), BF16),
            vmem((2, T, HD), BF16),
            vmem((2, T, HD), BF16),
            vmem((nz, 2, 2, T, HD), BF16),
            vmem((ny, 2, 2, T, HD), BF16),
            vmem((pairs, T), F32),
            vmem((nz, B, T), F32),
            vmem((ny, B), F32),
            vmem((nz, ny, B, B), F32),
            vmem((nz, ny, B, B), F32),
            vmem((nz, HD, B), BF16),
            vmem((nz, ny, B), F32),
            vmem((nz, ny, B), F32),
            vmem((nz, ny, B), F32),
            vmem((ny, 3, ny, B), F32),
            vmem((nz, ny, B), F32),
            vmem((ny, ny, B), F32),
            vmem((ny, B), F32),
            vmem((ny, HD, B), BF16),
            vmem((ny, HD, B), BF16),
            vmem((2, ny, HD, B), BF16),
            vmem((ny, 2, T, cols), BF16),
            vmem((nz, zcols, 2 * HD), F32),
            vmem((nz, zcols, 2 * HD), F32),
            vmem((nz, B, HD), F32),
            vmem((nz, B, HD), F32),
            vmem((ny, HD, B), F32),
            vmem((2, half, 2, T, HD), BF16),
            vmem((2, half, 2, T, HD), BF16),
            vmem((2, half, 2, T, HD), F32),
            vmem((2, half, 2, T, HD), F32),
            vmem((ny, 2, HD, T), BF16),
            vmem((2, ny, HD, T), BF16),
            vmem((T, HD), F32),
            vmem((T, HD), F32),
            vmem((T, HD), BF16),
            vmem((T, HD), BF16),
            dma((7,)),
            dma((160,)),
            dma((nz, 2)),
            dma((ny, 2)),
            dma((2, ny)),
            dma((ny,)),
            dma((ny,)),
            dma((2, ny)),
            dma((nz,)),
            dma((3, 2, half, 2)),
            dma((2, ny)),
            dma((2,)),
        ],
        compiler_params=pltpu.CompilerParams(
            collective_id=0, has_side_effects=True, vmem_limit_bytes=63 * 1024 * 1024
        ),
    )(queries, keys, values, out_grad, w_out, frames_in, order_in)
    o, g = results
    return o[:, :B], o[:, B:2*B], o[:, 2*B:], jnp.transpose(g)


def solution(mesh):
    ny, nz = {64: (4, 8), 32: (2, 8), 16: (2, 4)}[mesh.shape["ctx"]]
    placed = (
        P("ctx", "tp"),
        P("ctx", "tp"),
        P("ctx", "tp"),
        P("ctx", None),
        P("tp", None),
        P(),
        P(),
    )
    return jax.shard_map(
        functools.partial(shards, ny, nz),
        mesh=mesh,
        in_specs=placed,
        out_specs=(P("ctx", "tp"), P("ctx", "tp"), P("ctx", "tp"), P("tp", "ctx")),
        check_vma=False,
    )
```

```python
import functools
import math

import jax
import jax.numpy as jnp
from jax import lax
from jax.experimental import pallas as pl
from jax.experimental.pallas import tpu as pltpu
from jax.sharding import PartitionSpec as P

HD = 128
T = 128
B = 2 * T
MASKED = -1e30
FLOOR = -1e29
SCALE = HD**-0.5
EXP2_SCALE = SCALE * math.log2(math.e)
F32 = jnp.float32
BF16 = jnp.bfloat16
NT = (((1,), (1,)), ((), ()))
TN = (((0,), (0,)), ((), ()))
MESH = pl.DeviceIdType.MESH


def dot(a, b):
    return jnp.dot(a, b, preferred_element_type=F32)


def dot_general(a, b, dims):
    return lax.dot_general(a, b, dims, preferred_element_type=F32)


def kernel(
    ny,
    nz,
    q_hbm,
    k_hbm,
    v_hbm,
    og_hbm,
    w_hbm,
    fi_hbm,
    go_hbm,
    out_ref,
    gw_ref,
    q_in,
    k_in,
    v_in,
    og_in,
    w_in,
    fi_in,
    go_in,
    da,
    kv_other,
    qd_other,
    kv,
    qd,
    frames,
    kf,
    qf,
    wts,
    dps,
    v_t,
    mst,
    lst,
    dst,
    stats,
    cst,
    ysh,
    dlt,
    osend,
    orecv,
    att,
    ogb,
    gsend,
    grecv,
    acc_k,
    acc_v,
    acc_q,
    rsk_out,
    rsk_in,
    rsv_out,
    rsv_in,
    qsend,
    qrecv,
    finv_out,
    finv_in,
    fink_out,
    fink_in,
    in_sem,
    sent,
    z_r,
    y_r,
    og_r,
    st_r,
    o_r,
    att_r,
    g_r,
    rs_r,
    dq_r,
    fin_r,
):
    gq_ref, gk_ref, gv_ref = (out_ref.at[:, pl.ds(i * B, B)] for i in range(3))
    half = nz // 2
    me = lax.axis_index("ctx")
    x = me // (ny * nz)
    y = lax.rem(me // nz, ny)
    z = lax.rem(me, nz)
    px = 1 - x
    cols = og_in.shape[1] // (2 * ny)
    zcols = cols // nz

    def at(xx, yy, zz):
        return xx * (ny * nz) + yy * nz + zz

    partner = at(px, y, z)
    right = at(x, y, lax.rem(z + 1, nz))
    left = at(x, y, lax.rem(z + nz - 1, nz))
    ypos = [lax.rem(y + k, ny) for k in range(ny)]
    ypeer = [at(x, ypos[k], z) for k in range(ny)]
    ydiag = [at(px, ypos[k], z) for k in range(ny)]
    zpos = [lax.rem(z + k, nz) for k in range(nz)]
    zpeer = [at(x, y, zpos[k]) for k in range(nz)]
    zdiag = [at(px, y, zpos[k]) for k in range(nz)]

    started = []

    def send(src, dst_ref, r_sem, device):
        copy = pltpu.make_async_remote_copy(
            src_ref=src,
            dst_ref=dst_ref,
            send_sem=sent.at[len(started)],
            recv_sem=r_sem,
            device_id={"ctx": device},
            device_id_type=MESH,
        )
        copy.start()
        started.append(copy)

    def arrived(dst_ref, r_sem):
        pltpu.make_async_remote_copy(
            src_ref=dst_ref,
            dst_ref=dst_ref,
            send_sem=sent.at[0],
            recv_sem=r_sem,
            device_id={"ctx": partner},
            device_id_type=MESH,
        ).wait_recv()

    loads = [
        pltpu.make_async_copy(src, to, in_sem.at[i])
        for i, (src, to) in enumerate(
            [
                (k_hbm, k_in),
                (v_hbm, v_in),
                (w_hbm, w_in),
                (og_hbm, og_in),
                (q_hbm, q_in),
                (fi_hbm, fi_in),
                (go_hbm, go_in),
            ]
        )
    ]
    for load in loads:
        load.start()
    barrier = pltpu.get_barrier_semaphore()
    peers = ydiag + ypeer[1:] + zpeer[1:] + [zdiag[1], zdiag[nz - 1]]
    for peer in peers:
        pl.semaphore_signal(barrier, inc=1, device_id={"ctx": peer}, device_id_type=MESH)
    own_lanes = pl.ds(pl.multiple_of(x * HD, HD), HD)
    other_lanes = pl.ds(pl.multiple_of(px * HD, HD), HD)

    def stage(src, own, other, i):
        own[i] = src[:, own_lanes]
        other[i] = src[:, other_lanes]

    for load in loads:
        load.wait()
    stage(k_in, kv.at[0, 0], kv_other, 0)
    stage(v_in, kv.at[0, 0], kv_other, 1)
    da[...] = dot_general(og_in[...], w_in[...], NT).astype(BF16)
    stage(q_in, qd.at[y, 0], qd_other, 0)
    stage(da, qd.at[y, 0], qd_other, 1)

    go = go_in[...]
    fi = fi_in[...].astype(F32)
    pairs, lanes = fi.shape
    groups = go.shape[1]
    half_lanes = lanes // 2
    lane = lax.broadcasted_iota(jnp.int32, (pairs, lanes), 1)
    low = jnp.where(lane < half_lanes, fi, 0.0)
    high = jnp.where(lane >= half_lanes, fi, 0.0)
    low_up = jnp.concatenate([low[:, half_lanes:], low[:, :half_lanes]], axis=1)
    high_down = jnp.concatenate([high[:, half_lanes:], high[:, :half_lanes]], axis=1)
    row = lax.broadcasted_iota(jnp.int32, (pairs, groups), 0)
    holds = [(go == 2 * row + p).astype(F32).astype(BF16) for p in range(2)]
    group_id = lax.broadcasted_iota(jnp.int32, (groups, pairs), 0)
    pair_id = lax.broadcasted_iota(jnp.int32, (groups, pairs), 1)
    picks = [(group_id == 2 * pair_id + e).astype(F32).astype(BF16) for e in range(2)]
    total = jnp.zeros((pairs, lanes), F32)
    for p in range(2):
        for e in range(2):
            part = ((low, low_up), (high_down, high))[p][e]
            total += dot_general(dot(holds[p], picks[e]).astype(BF16), part.astype(BF16), TN)
    frames[...] = total
    across = jnp.transpose(total)
    device_lane = lax.broadcasted_iota(jnp.int32, (lanes, pairs), 1)
    distance = (
        [0] + [nz - s for s in range(1, half)] + [s for s in range(1, half)] + [half]
    )
    for slot in range(nz):
        for c in range(2):
            source = at(x if c == 0 else px, y, zpos[distance[slot]])
            column = jnp.sum(jnp.where(device_lane == source, across, 0.0), axis=1, keepdims=True)
            kf[slot, pl.ds(c * T, T), :] = jnp.broadcast_to(column, (T, lanes))
    for b in range(ny):
        qf[pl.ds(b, 1), pl.ds(0, T)] = frames[pl.ds(at(x, b, z), 1), :]
        qf[pl.ds(b, 1), pl.ds(T, T)] = frames[pl.ds(at(px, b, z), 1), :]

    pl.semaphore_wait(barrier, len(peers))

    def left_slot(s):
        return s if s < half else nz - 1

    def right_slot(s):
        return half - 1 + s if s < half else nz - 1

    def z_send(way, s, c):
        slots = (left_slot, right_slot)[way]
        k = 1 if way == 0 else nz - 1
        slot = slots(s)
        if s > 1:
            send(kv.at[slots(s - 1), c], kv.at[slot, c], z_r.at[slot, c], zpeer[k])
        elif c == 0:
            send(kv.at[0, 0], kv.at[slot, 0], z_r.at[slot, 0], zpeer[k])
        else:
            send(kv_other, kv.at[slot, 1], z_r.at[slot, 1], zdiag[k])

    def z_arrived(slot, c):
        arrived(kv.at[slot, c], z_r.at[slot, c])

    def z_send_far(way, source, peers_far):
        k = 2 if way == 0 else nz - 2
        send(source, kv.at[nz - 1, way], z_r.at[nz - 1, way], peers_far[k])

    def relay(s):
        for c in range(2):
            for way in range(2):
                slot = (left_slot, right_slot)[way](s)
                z_arrived(slot, c)
                if s + 1 < half:
                    z_send(way, s + 1, c)
                if s == half - 2 and way == c:
                    z_send_far(way, kv.at[slot, c], zpeer)

    for c in range(2):
        for way in range(2):
            z_send(way, 1, c)
    if half == 2:
        z_send_far(0, kv.at[0, 0], zpeer)
        z_send_far(1, kv_other, zdiag)
    for k in range(1, ny):
        send(qd.at[y, 0], qd.at[y, 0], y_r.at[ny - k, 0], ypeer[k])
    for k in range(ny):
        send(qd_other, qd.at[y, 1], y_r.at[(ny - k) % ny, 1], ydiag[k])
    send(kv_other, kv.at[0, 1], z_r.at[0, 1], partner)

    def og_lanes(xx, yy):
        return pl.ds(pl.multiple_of((xx * ny + yy) * cols, cols), cols)

    og_targets = [(x, k, ypeer[k]) for k in range(1, ny)] + [(px, k, ydiag[k]) for k in range(ny)]

    def og_send():
        ogb[y, x] = og_in[:, og_lanes(x, y)]
        for i, (xx, k, device) in enumerate(og_targets):
            side = 0 if i < ny - 1 else 1
            r = (ny - k) % ny
            send(
                og_in.at[:, og_lanes(xx, ypos[k])],
                ogb.at[y, x],
                og_r.at[side, r],
                device,
            )

    def forward(slot):
        kb = kv[slot, :, 0].reshape(B, HD)
        vb = kv[slot, :, 1].reshape(B, HD)
        v_t[slot] = jnp.transpose(vb)
        key_frames = jnp.concatenate([kf[slot], kf[slot]], axis=1)

        def body(b, carry):
            scores = dot_general(kb, qd[b, :, 0].reshape(B, HD), NT)
            grads = dot_general(vb, qd[b, :, 1].reshape(B, HD), NT)
            scores = jnp.where(key_frames <= qf[pl.ds(b, 1), :], scores, MASKED)
            top = jnp.maximum(jnp.max(scores, axis=0, keepdims=True), FLOOR)
            weights = jnp.exp2((scores - top) * EXP2_SCALE)
            wts[slot, b] = weights
            dps[slot, b] = grads
            mst[slot, pl.ds(b, 1), :] = top
            lst[slot, pl.ds(b, 1), :] = jnp.sum(weights, axis=0, keepdims=True)
            dst[slot, pl.ds(b, 1), :] = jnp.sum(weights * grads, axis=0, keepdims=True)
            return carry

        lax.fori_loop(0, ny, body, 0, unroll=True)

    for s in range(1, max(half - 1, 2)):
        relay(s)
    z_arrived(0, 1)
    for k in range(ny):
        for c in range(2):
            if k + c > 0:
                arrived(qd.at[ypos[k], c], y_r.at[k, c])
    og_send()
    forward(0)
    for s in range(1, half):
        if s > 1 and s == half - 1:
            relay(s)
        forward(left_slot(s))
        forward(right_slot(s))
    z_arrived(nz - 1, 0)
    z_arrived(nz - 1, 1)
    forward(nz - 1)

    tops = mst[...]
    own_top = jnp.max(tops, axis=0)
    shares = jnp.exp2((tops - own_top[None]) * EXP2_SCALE)
    stats[y, 0] = own_top
    stats[y, 1] = jnp.sum(shares * lst[...], axis=0)
    stats[y, 2] = jnp.sum(shares * dst[...], axis=0)
    for k in sorted(range(1, ny), key=lambda k: -min(k, ny - k)):
        send(stats.at[y], stats.at[y], st_r.at[ny - k], ypeer[k])

    cst[...] = shares

    for k in [*range(1, ny), 0]:
        b = ypos[k]
        part = jnp.zeros((HD, B), F32)
        for slot in range(nz):
            part += dot(v_t[slot], (wts[slot, b] * cst[slot, pl.ds(b, 1), :]).astype(BF16))
        osend[b] = part.astype(BF16)
        if k > 0:
            send(osend.at[b], orecv.at[ny - k], o_r.at[ny - k], ypeer[k])

    for k in range(1, ny):
        arrived(stats.at[ypos[k]], st_r.at[k])
    all_top = stats[0, 0]
    for b in range(1, ny):
        all_top = jnp.maximum(all_top, stats[b, 0])
    row_total = jnp.zeros_like(all_top)
    delta = jnp.zeros_like(all_top)
    for b in range(ny):
        share = jnp.exp2((stats[b, 0] - all_top) * EXP2_SCALE)
        row_total += share * stats[b, 1]
        delta += share * stats[b, 2]
        ysh[b] = share
    inverse = 1.0 / row_total
    for b in range(ny):
        ysh[b] = ysh[b] * inverse
    dlt[...] = delta * inverse
    cst[...] = jnp.exp2((tops - all_top[None]) * EXP2_SCALE) * inverse[None]

    acc_q[...] = jnp.zeros_like(acc_q)

    def backward(slot):
        k_t = jnp.transpose(kv[slot, :, 0].reshape(B, HD))
        acc_k[slot] = jnp.zeros((B, HD), F32)
        acc_v[slot] = jnp.zeros((B, HD), F32)

        def body(b, carry):
            probs = wts[slot, b] * cst[slot, pl.ds(b, 1), :]
            grad_scores = (probs * (dps[slot, b] - dlt[pl.ds(b, 1), :])).astype(BF16)
            acc_v[slot] += dot(probs.astype(BF16), qd[b, :, 1].reshape(B, HD))
            acc_k[slot] += dot(grad_scores, qd[b, :, 0].reshape(B, HD))
            acc_q[b] += dot(k_t, grad_scores)
            return carry

        lax.fori_loop(0, ny, body, 0, unroll=True)

    pieces = (
        (0, T, acc_v, rsv_out, rsv_in),
        (0, T, acc_k, rsk_out, rsk_in),
    )

    def reduce_send(way, step, c, t, arrival):
        d = half + 1 - step
        i = step - 1
        slot = (right_slot, left_slot)[way](d)
        k = 1 if way == 0 else nz - 1
        device = zdiag[k] if step == half and c == 1 else zpeer[k]
        first, count, acc, src, to = pieces[t]
        rows = pl.ds(first, count)
        part = acc[slot, pl.ds(c * T + first, count), :]
        if arrival:
            arrived(to.at[way, i - 1, c, rows], rs_r.at[t, way, i - 1, c])
            part += to[way, i - 1, c, rows].astype(F32)
        src[way, i, c, rows] = part.astype(src.dtype)
        send(src.at[way, i, c, rows], to.at[way, i, c, rows], rs_r.at[t, way, i, c], device)

    def reduce_chunk(way, step, c):
        for t in range(2):
            reduce_send(way, step, c, t, False)

    def reduce_rest(step):
        for turn in range(2 if step > 2 else 1):
            for t in range(2):
                for way in range(2):
                    last = turn == 1 or step == 2
                    reduce_send(way, step, way if last else 1 - way, t, True)

    def attended_rows():
        for k in range(1, ny):
            arrived(orecv.at[k], o_r.at[k])
        rows_att = osend[y].astype(F32) * ysh[y, pl.ds(y, 1), :]
        for k in range(1, ny):
            rows_att += orecv[k].astype(F32) * ysh[ypos[k], pl.ds(y, 1), :]
        att[x, y] = rows_att.astype(BF16)
        for i, (xx, k, device) in enumerate(og_targets):
            side = 0 if i < ny - 1 else 1
            send(att.at[x, y], att.at[x, y], att_r.at[side, (ny - k) % ny], device)

    def query_part():
        backward(0)
        for t, (acc, src, to) in enumerate(((acc_v, finv_out, finv_in), (acc_k, fink_out, fink_in))):
            src[...] = acc[0, pl.ds(T, T), :].astype(src.dtype)
            send(src, to, fin_r.at[t], partner)
        for b in range(ny):
            for c in range(2):
                qsend[b, c] = acc_q[b, :, pl.ds(c * T, T)].astype(BF16)
        for k in range(ny):
            r = (ny - k) % ny
            if k > 0:
                send(qsend.at[ypos[k], 0], qrecv.at[0, r], dq_r.at[0, r], ypeer[k])
            send(qsend.at[ypos[k], 1], qrecv.at[1, r], dq_r.at[1, r], ydiag[k])

    def weight_part():
        for i, (xx, k, device) in enumerate(og_targets):
            side = 0 if i < ny - 1 else 1
            source_x = x if side == 0 else px
            arrived(ogb.at[ypos[k], source_x], og_r.at[side, k])
            arrived(att.at[source_x, ypos[k]], att_r.at[side, k])
        for h in range(2):
            part = jnp.zeros((HD, cols), F32)
            for b in range(ny):
                for c in range(2):
                    part += dot(att[h, b, :, pl.ds(c * T, T)], ogb[b, h ^ c])
            gsend[:, :, pl.ds(h * HD, HD)] = jnp.transpose(part).reshape(nz, zcols, HD)
        for k in range(1, nz):
            send(gsend.at[zpos[k]], grecv.at[nz - k], g_r.at[nz - k], zpeer[k])

    backward(nz - 1)
    reduce_chunk(0, 1, 0)
    reduce_chunk(1, 1, 1)
    backward(right_slot(half - 1))
    reduce_chunk(0, 2, 1)
    backward(left_slot(half - 1))
    reduce_chunk(1, 2, 0)
    attended_rows()
    for d in range(half - 2, 0, -1):
        backward(right_slot(d))
        backward(left_slot(d))
    for step in range(2, half + 1):
        if step == max(half, 3):
            weight_part()
        reduce_rest(step)
        if step == 2:
            query_part()
    if half == 2:
        weight_part()

    for t, (acc, src, to) in enumerate(((acc_v, finv_out, finv_in), (acc_k, fink_out, fink_in))):
        arrived(to, fin_r.at[t])
    for k in range(ny):
        for c in range(2):
            if k + c > 0:
                arrived(qrecv.at[c, k], dq_r.at[c, k])
    for c, lanes_out in enumerate((own_lanes, other_lanes)):
        rows_q = qsend[y, 0].astype(F32) if c == 0 else qrecv[1, 0].astype(F32)
        for k in range(1, ny):
            rows_q += qrecv[c, k].astype(F32)
        gq_ref[:, lanes_out] = jnp.transpose(rows_q * SCALE).astype(BF16)
    for c, lanes_out in ((1, other_lanes), (0, own_lanes)):
        part_v = finv_in[...] if c == 1 else acc_v[0, pl.ds(0, T), :]
        part_k = fink_in[...].astype(F32) if c == 1 else acc_k[0, pl.ds(0, T), :]
        for way in (0, 1) if c == 1 else (1, 0):
            for t, (first, count, acc, src, to) in enumerate(pieces):
                arrived(to.at[way, half - 1, c, pl.ds(first, count)], rs_r.at[t, way, half - 1, c])
            part_v += rsv_in[way, half - 1, c]
            part_k += rsk_in[way, half - 1, c].astype(F32)
        gv_ref[:, lanes_out] = part_v.astype(BF16)
        gk_ref[:, lanes_out] = (part_k * SCALE).astype(BF16)

    for k in range(1, nz):
        arrived(grecv.at[k], g_r.at[k])
    weight_rows = gsend[z]
    for k in range(1, nz):
        weight_rows += grecv[k]
    gw_ref[...] = weight_rows

    for copy in started:
        copy.wait_send()


def shards(ny, nz, queries, keys, values, out_grad, w_out, frame_index, group_order):
    half = nz // 2
    width = out_grad.shape[1]
    cols = width // (2 * ny)
    zcols = cols // nz
    pairs = group_order.shape[0] // 2
    frames_in = frame_index.reshape(pairs, T)
    order_in = group_order.reshape(1, 2 * pairs)
    vmem = pltpu.VMEM
    dma = pltpu.SemaphoreType.DMA
    any_spec = pl.BlockSpec(memory_space=pltpu.HBM)
    out_spec = pl.BlockSpec(memory_space=pltpu.VMEM)
    results = pl.pallas_call(
        functools.partial(kernel, ny, nz),
        out_shape=(
            jax.ShapeDtypeStruct((T, 6 * HD), BF16),
            jax.ShapeDtypeStruct((zcols, 2 * HD), F32),
        ),
        in_specs=[any_spec] * 7,
        out_specs=(out_spec,) * 2,
        scratch_shapes=[
            vmem((T, 2 * HD), BF16),
            vmem((T, 2 * HD), BF16),
            vmem((T, 2 * HD), BF16),
            vmem((T, width), BF16),
            vmem((2 * HD, width), BF16),
            vmem((pairs, T), jnp.int32),
            vmem((1, 2 * pairs), jnp.int32),
            vmem((T, 2 * HD), BF16),
            vmem((2, T, HD), BF16),
            vmem((2, T, HD), BF16),
            vmem((nz, 2, 2, T, HD), BF16),
            vmem((ny, 2, 2, T, HD), BF16),
            vmem((pairs, T), F32),
            vmem((nz, B, T), F32),
            vmem((ny, B), F32),
            vmem((nz, ny, B, B), F32),
            vmem((nz, ny, B, B), F32),
            vmem((nz, HD, B), BF16),
            vmem((nz, ny, B), F32),
            vmem((nz, ny, B), F32),
            vmem((nz, ny, B), F32),
            vmem((ny, 3, ny, B), F32),
            vmem((nz, ny, B), F32),
            vmem((ny, ny, B), F32),
            vmem((ny, B), F32),
            vmem((ny, HD, B), BF16),
            vmem((ny, HD, B), BF16),
            vmem((2, ny, HD, B), BF16),
            vmem((ny, 2, T, cols), BF16),
            vmem((nz, zcols, 2 * HD), F32),
            vmem((nz, zcols, 2 * HD), F32),
            vmem((nz, B, HD), F32),
            vmem((nz, B, HD), F32),
            vmem((ny, HD, B), F32),
            vmem((2, half, 2, T, HD), BF16),
            vmem((2, half, 2, T, HD), BF16),
            vmem((2, half, 2, T, HD), F32),
            vmem((2, half, 2, T, HD), F32),
            vmem((ny, 2, HD, T), BF16),
            vmem((2, ny, HD, T), BF16),
            vmem((T, HD), F32),
            vmem((T, HD), F32),
            vmem((T, HD), BF16),
            vmem((T, HD), BF16),
            dma((7,)),
            dma((160,)),
            dma((nz, 2)),
            dma((ny, 2)),
            dma((2, ny)),
            dma((ny,)),
            dma((ny,)),
            dma((2, ny)),
            dma((nz,)),
            dma((3, 2, half, 2)),
            dma((2, ny)),
            dma((2,)),
        ],
        compiler_params=pltpu.CompilerParams(
            collective_id=0, has_side_effects=True, vmem_limit_bytes=63 * 1024 * 1024
        ),
    )(queries, keys, values, out_grad, w_out, frames_in, order_in)
    o, g = results
    return o[:, :B], o[:, B:2*B], o[:, 2*B:], jnp.transpose(g)


def solution(mesh):
    ny, nz = {64: (4, 8), 32: (2, 8), 16: (2, 4)}[mesh.shape["ctx"]]
    placed = (
        P("ctx", "tp"),
        P("ctx", "tp"),
        P("ctx", "tp"),
        P("ctx", None),
        P("tp", None),
        P(),
        P(),
    )
    return jax.shard_map(
        functools.partial(shards, ny, nz),
        mesh=mesh,
        in_specs=placed,
        out_specs=(P("ctx", "tp"), P("ctx", "tp"), P("ctx", "tp"), P("tp", "ctx")),
        check_vma=False,
    )
```

```python
import functools
import math

import jax
import jax.numpy as jnp
from jax import lax
from jax.experimental import pallas as pl
from jax.experimental.pallas import tpu as pltpu
from jax.sharding import PartitionSpec as P

HD = 128
T = 128
B = 2 * T
MASKED = -1e30
FLOOR = -1e29
SCALE = HD**-0.5
EXP2_SCALE = SCALE * math.log2(math.e)
F32 = jnp.float32
BF16 = jnp.bfloat16
NT = (((1,), (1,)), ((), ()))
TN = (((0,), (0,)), ((), ()))
MESH = pl.DeviceIdType.MESH


def dot(a, b):
    return jnp.dot(a, b, preferred_element_type=F32)


def dot_general(a, b, dims):
    return lax.dot_general(a, b, dims, preferred_element_type=F32)


def kernel(
    ny,
    nz,
    q_hbm,
    k_hbm,
    v_hbm,
    og_hbm,
    w_hbm,
    fi_hbm,
    go_hbm,
    out_ref,
    gw_ref,
    q_in,
    k_in,
    v_in,
    og_in,
    w_in,
    fi_in,
    go_in,
    da,
    kv_other,
    qd_other,
    kv,
    qd,
    frames,
    kf,
    qf,
    wts,
    dps,
    v_t,
    mst,
    lst,
    dst,
    stats,
    cst,
    ysh,
    dlt,
    osend,
    orecv,
    att,
    ogb,
    gsend,
    grecv,
    acc_k,
    acc_v,
    acc_q,
    rsk_out,
    rsk_in,
    rsv_out,
    rsv_in,
    qsend,
    qrecv,
    finv_out,
    finv_in,
    fink_out,
    fink_in,
    in_sem,
    sent,
    z_r,
    y_r,
    og_r,
    st_r,
    o_r,
    att_r,
    g_r,
    rs_r,
    dq_r,
    fin_r,
):
    gq_ref, gk_ref, gv_ref = (out_ref.at[:, pl.ds(i * B, B)] for i in range(3))
    half = nz // 2
    me = lax.axis_index("ctx")
    x = me // (ny * nz)
    y = lax.rem(me // nz, ny)
    z = lax.rem(me, nz)
    px = 1 - x
    cols = og_in.shape[1] // (2 * ny)
    zcols = cols // nz

    def at(xx, yy, zz):
        return xx * (ny * nz) + yy * nz + zz

    partner = at(px, y, z)
    right = at(x, y, lax.rem(z + 1, nz))
    left = at(x, y, lax.rem(z + nz - 1, nz))
    ypos = [lax.rem(y + k, ny) for k in range(ny)]
    ypeer = [at(x, ypos[k], z) for k in range(ny)]
    ydiag = [at(px, ypos[k], z) for k in range(ny)]
    zpos = [lax.rem(z + k, nz) for k in range(nz)]
    zpeer = [at(x, y, zpos[k]) for k in range(nz)]
    zdiag = [at(px, y, zpos[k]) for k in range(nz)]

    started = []

    def send(src, dst_ref, r_sem, device):
        copy = pltpu.make_async_remote_copy(
            src_ref=src,
            dst_ref=dst_ref,
            send_sem=sent.at[len(started)],
            recv_sem=r_sem,
            device_id={"ctx": device},
            device_id_type=MESH,
        )
        copy.start()
        started.append(copy)

    def arrived(dst_ref, r_sem):
        pltpu.make_async_remote_copy(
            src_ref=dst_ref,
            dst_ref=dst_ref,
            send_sem=sent.at[0],
            recv_sem=r_sem,
            device_id={"ctx": partner},
            device_id_type=MESH,
        ).wait_recv()

    loads = [
        pltpu.make_async_copy(src, to, in_sem.at[i])
        for i, (src, to) in enumerate(
            [
                (k_hbm, k_in),
                (v_hbm, v_in),
                (w_hbm, w_in),
                (og_hbm, og_in),
                (q_hbm, q_in),
                (fi_hbm, fi_in),
                (go_hbm, go_in),
            ]
        )
    ]
    for load in loads:
        load.start()
    barrier = pltpu.get_barrier_semaphore()
    peers = ydiag + ypeer[1:] + zpeer[1:] + [zdiag[1], zdiag[nz - 1]]
    for peer in peers:
        pl.semaphore_signal(barrier, inc=1, device_id={"ctx": peer}, device_id_type=MESH)
    own_lanes = pl.ds(pl.multiple_of(x * HD, HD), HD)
    other_lanes = pl.ds(pl.multiple_of(px * HD, HD), HD)

    def stage(src, own, other, i):
        own[i] = src[:, own_lanes]
        other[i] = src[:, other_lanes]

    for load in loads:
        load.wait()
    stage(k_in, kv.at[0, 0], kv_other, 0)
    stage(v_in, kv.at[0, 0], kv_other, 1)
    da[...] = dot_general(og_in[...], w_in[...], NT).astype(BF16)
    stage(q_in, qd.at[y, 0], qd_other, 0)
    stage(da, qd.at[y, 0], qd_other, 1)

    go = go_in[...]
    fi = fi_in[...].astype(F32)
    pairs, lanes = fi.shape
    groups = go.shape[1]
    half_lanes = lanes // 2
    lane = lax.broadcasted_iota(jnp.int32, (pairs, lanes), 1)
    low = jnp.where(lane < half_lanes, fi, 0.0)
    high = jnp.where(lane >= half_lanes, fi, 0.0)
    low_up = jnp.concatenate([low[:, half_lanes:], low[:, :half_lanes]], axis=1)
    high_down = jnp.concatenate([high[:, half_lanes:], high[:, :half_lanes]], axis=1)
    row = lax.broadcasted_iota(jnp.int32, (pairs, groups), 0)
    holds = [(go == 2 * row + p).astype(F32).astype(BF16) for p in range(2)]
    group_id = lax.broadcasted_iota(jnp.int32, (groups, pairs), 0)
    pair_id = lax.broadcasted_iota(jnp.int32, (groups, pairs), 1)
    picks = [(group_id == 2 * pair_id + e).astype(F32).astype(BF16) for e in range(2)]
    total = jnp.zeros((pairs, lanes), F32)
    for p in range(2):
        for e in range(2):
            part = ((low, low_up), (high_down, high))[p][e]
            total += dot_general(dot(holds[p], picks[e]).astype(BF16), part.astype(BF16), TN)
    frames[...] = total
    across = jnp.transpose(total)
    device_lane = lax.broadcasted_iota(jnp.int32, (lanes, pairs), 1)
    distance = (
        [0] + [nz - s for s in range(1, half)] + [s for s in range(1, half)] + [half]
    )
    for slot in range(nz):
        for c in range(2):
            source = at(x if c == 0 else px, y, zpos[distance[slot]])
            column = jnp.sum(jnp.where(device_lane == source, across, 0.0), axis=1, keepdims=True)
            kf[slot, pl.ds(c * T, T), :] = jnp.broadcast_to(column, (T, lanes))
    for b in range(ny):
        qf[pl.ds(b, 1), pl.ds(0, T)] = frames[pl.ds(at(x, b, z), 1), :]
        qf[pl.ds(b, 1), pl.ds(T, T)] = frames[pl.ds(at(px, b, z), 1), :]

    pl.semaphore_wait(barrier, len(peers))

    def left_slot(s):
        return s if s < half else nz - 1

    def right_slot(s):
        return half - 1 + s if s < half else nz - 1

    def z_send(way, s, c):
        slots = (left_slot, right_slot)[way]
        k = 1 if way == 0 else nz - 1
        slot = slots(s)
        if s > 1:
            send(kv.at[slots(s - 1), c], kv.at[slot, c], z_r.at[slot, c], zpeer[k])
        elif c == 0:
            send(kv.at[0, 0], kv.at[slot, 0], z_r.at[slot, 0], zpeer[k])
        else:
            send(kv_other, kv.at[slot, 1], z_r.at[slot, 1], zdiag[k])

    def z_arrived(slot, c):
        arrived(kv.at[slot, c], z_r.at[slot, c])

    def z_send_far(way, source, peers_far):
        k = 2 if way == 0 else nz - 2
        send(source, kv.at[nz - 1, way], z_r.at[nz - 1, way], peers_far[k])

    def relay(s):
        for c in range(2):
            for way in range(2):
                slot = (left_slot, right_slot)[way](s)
                z_arrived(slot, c)
                if s + 1 < half:
                    z_send(way, s + 1, c)
                if s == half - 2 and way == c:
                    z_send_far(way, kv.at[slot, c], zpeer)

    for c in range(2):
        for way in range(2):
            z_send(way, 1, c)
    if half == 2:
        z_send_far(0, kv.at[0, 0], zpeer)
        z_send_far(1, kv_other, zdiag)
    for k in range(1, ny):
        send(qd.at[y, 0], qd.at[y, 0], y_r.at[ny - k, 0], ypeer[k])
    for k in range(ny):
        send(qd_other, qd.at[y, 1], y_r.at[(ny - k) % ny, 1], ydiag[k])
    send(kv_other, kv.at[0, 1], z_r.at[0, 1], partner)

    def og_lanes(xx, yy):
        return pl.ds(pl.multiple_of((xx * ny + yy) * cols, cols), cols)

    og_targets = [(x, k, ypeer[k]) for k in range(1, ny)] + [(px, k, ydiag[k]) for k in range(ny)]

    def og_send():
        ogb[y, x] = og_in[:, og_lanes(x, y)]
        for i, (xx, k, device) in enumerate(og_targets):
            side = 0 if i < ny - 1 else 1
            r = (ny - k) % ny
            send(
                og_in.at[:, og_lanes(xx, ypos[k])],
                ogb.at[y, x],
                og_r.at[side, r],
                device,
            )

    def forward(slot):
        kb = kv[slot, :, 0].reshape(B, HD)
        vb = kv[slot, :, 1].reshape(B, HD)
        v_t[slot] = jnp.transpose(vb)
        key_frames = jnp.concatenate([kf[slot], kf[slot]], axis=1)

        def body(b, carry):
            scores = dot_general(kb, qd[b, :, 0].reshape(B, HD), NT)
            grads = dot_general(vb, qd[b, :, 1].reshape(B, HD), NT)
            scores = jnp.where(key_frames <= qf[pl.ds(b, 1), :], scores, MASKED)
            top = jnp.maximum(jnp.max(scores, axis=0, keepdims=True), FLOOR)
            weights = jnp.exp2((scores - top) * EXP2_SCALE)
            wts[slot, b] = weights
            dps[slot, b] = grads
            mst[slot, pl.ds(b, 1), :] = top
            lst[slot, pl.ds(b, 1), :] = jnp.sum(weights, axis=0, keepdims=True)
            dst[slot, pl.ds(b, 1), :] = jnp.sum(weights * grads, axis=0, keepdims=True)
            return carry

        lax.fori_loop(0, ny, body, 0, unroll=True)

    for s in range(1, max(half - 1, 2)):
        relay(s)
    z_arrived(0, 1)
    for k in range(ny):
        for c in range(2):
            if k + c > 0:
                arrived(qd.at[ypos[k], c], y_r.at[k, c])
    og_send()
    forward(0)
    for s in range(1, half):
        if s > 1 and s == half - 1:
            relay(s)
        forward(left_slot(s))
        forward(right_slot(s))
    z_arrived(nz - 1, 0)
    z_arrived(nz - 1, 1)
    forward(nz - 1)

    tops = mst[...]
    own_top = jnp.max(tops, axis=0)
    shares = jnp.exp2((tops - own_top[None]) * EXP2_SCALE)
    stats[y, 0] = own_top
    stats[y, 1] = jnp.sum(shares * lst[...], axis=0)
    stats[y, 2] = jnp.sum(shares * dst[...], axis=0)
    for k in sorted(range(1, ny), key=lambda k: -min(k, ny - k)):
        send(stats.at[y], stats.at[y], st_r.at[ny - k], ypeer[k])

    cst[...] = shares

    for k in sorted(range(ny), key=lambda k: -min(k, ny - k)):
        b = ypos[k]
        part = jnp.zeros((HD, B), F32)
        for slot in range(nz):
            part += dot(v_t[slot], (wts[slot, b] * cst[slot, pl.ds(b, 1), :]).astype(BF16))
        osend[b] = part.astype(BF16)
        if k > 0:
            send(osend.at[b], orecv.at[ny - k], o_r.at[ny - k], ypeer[k])

    for k in range(1, ny):
        arrived(stats.at[ypos[k]], st_r.at[k])
    all_top = stats[0, 0]
    for b in range(1, ny):
        all_top = jnp.maximum(all_top, stats[b, 0])
    row_total = jnp.zeros_like(all_top)
    delta = jnp.zeros_like(all_top)
    for b in range(ny):
        share = jnp.exp2((stats[b, 0] - all_top) * EXP2_SCALE)
        row_total += share * stats[b, 1]
        delta += share * stats[b, 2]
        ysh[b] = share
    inverse = 1.0 / row_total
    for b in range(ny):
        ysh[b] = ysh[b] * inverse
    dlt[...] = delta * inverse
    cst[...] = jnp.exp2((tops - all_top[None]) * EXP2_SCALE) * inverse[None]

    acc_q[...] = jnp.zeros_like(acc_q)

    def backward(slot):
        k_t = jnp.transpose(kv[slot, :, 0].reshape(B, HD))
        acc_k[slot] = jnp.zeros((B, HD), F32)
        acc_v[slot] = jnp.zeros((B, HD), F32)

        def body(b, carry):
            probs = wts[slot, b] * cst[slot, pl.ds(b, 1), :]
            grad_scores = (probs * (dps[slot, b] - dlt[pl.ds(b, 1), :])).astype(BF16)
            acc_v[slot] += dot(probs.astype(BF16), qd[b, :, 1].reshape(B, HD))
            acc_k[slot] += dot(grad_scores, qd[b, :, 0].reshape(B, HD))
            acc_q[b] += dot(k_t, grad_scores)
            return carry

        lax.fori_loop(0, ny, body, 0, unroll=True)

    pieces = (
        (0, T, acc_v, rsv_out, rsv_in),
        (0, T, acc_k, rsk_out, rsk_in),
    )

    def reduce_send(way, step, c, t, arrival):
        d = half + 1 - step
        i = step - 1
        slot = (right_slot, left_slot)[way](d)
        k = 1 if way == 0 else nz - 1
        device = zdiag[k] if step == half and c == 1 else zpeer[k]
        first, count, acc, src, to = pieces[t]
        rows = pl.ds(first, count)
        part = acc[slot, pl.ds(c * T + first, count), :]
        if arrival:
            arrived(to.at[way, i - 1, c, rows], rs_r.at[t, way, i - 1, c])
            part += to[way, i - 1, c, rows].astype(F32)
        src[way, i, c, rows] = part.astype(src.dtype)
        send(src.at[way, i, c, rows], to.at[way, i, c, rows], rs_r.at[t, way, i, c], device)

    def reduce_chunk(way, step, c):
        for t in range(2):
            reduce_send(way, step, c, t, False)

    def reduce_rest(step):
        for turn in range(2 if step > 2 else 1):
            for t in range(2):
                for way in range(2):
                    last = turn == 1 or step == 2
                    reduce_send(way, step, way if last else 1 - way, t, True)

    def attended_rows():
        for k in range(1, ny):
            arrived(orecv.at[k], o_r.at[k])
        rows_att = osend[y].astype(F32) * ysh[y, pl.ds(y, 1), :]
        for k in range(1, ny):
            rows_att += orecv[k].astype(F32) * ysh[ypos[k], pl.ds(y, 1), :]
        att[x, y] = rows_att.astype(BF16)
        for i, (xx, k, device) in enumerate(og_targets):
            side = 0 if i < ny - 1 else 1
            send(att.at[x, y], att.at[x, y], att_r.at[side, (ny - k) % ny], device)

    def query_part():
        backward(0)
        for t, (acc, src, to) in enumerate(((acc_v, finv_out, finv_in), (acc_k, fink_out, fink_in))):
            src[...] = acc[0, pl.ds(T, T), :].astype(src.dtype)
            send(src, to, fin_r.at[t], partner)
        for b in range(ny):
            for c in range(2):
                qsend[b, c] = acc_q[b, :, pl.ds(c * T, T)].astype(BF16)
        for k in range(ny):
            r = (ny - k) % ny
            if k > 0:
                send(qsend.at[ypos[k], 0], qrecv.at[0, r], dq_r.at[0, r], ypeer[k])
            send(qsend.at[ypos[k], 1], qrecv.at[1, r], dq_r.at[1, r], ydiag[k])

    def weight_part():
        for i, (xx, k, device) in enumerate(og_targets):
            side = 0 if i < ny - 1 else 1
            source_x = x if side == 0 else px
            arrived(ogb.at[ypos[k], source_x], og_r.at[side, k])
            arrived(att.at[source_x, ypos[k]], att_r.at[side, k])
        for h in range(2):
            part = jnp.zeros((HD, cols), F32)
            for b in range(ny):
                for c in range(2):
                    part += dot(att[h, b, :, pl.ds(c * T, T)], ogb[b, h ^ c])
            gsend[:, :, pl.ds(h * HD, HD)] = jnp.transpose(part).reshape(nz, zcols, HD)
        for k in sorted(range(1, nz), key=lambda k: -min(k, nz - k)):
            send(gsend.at[zpos[k]], grecv.at[nz - k], g_r.at[nz - k], zpeer[k])

    backward(nz - 1)
    reduce_chunk(0, 1, 0)
    reduce_chunk(1, 1, 1)
    backward(right_slot(half - 1))
    reduce_chunk(0, 2, 1)
    backward(left_slot(half - 1))
    reduce_chunk(1, 2, 0)
    attended_rows()
    for d in range(half - 2, 0, -1):
        backward(right_slot(d))
        backward(left_slot(d))
    for step in range(2, half + 1):
        if step == max(half, 3):
            weight_part()
        reduce_rest(step)
        if step == 2:
            query_part()
    if half == 2:
        weight_part()

    for t, (acc, src, to) in enumerate(((acc_v, finv_out, finv_in), (acc_k, fink_out, fink_in))):
        arrived(to, fin_r.at[t])
    for k in range(ny):
        for c in range(2):
            if k + c > 0:
                arrived(qrecv.at[c, k], dq_r.at[c, k])
    for c, lanes_out in enumerate((own_lanes, other_lanes)):
        rows_q = qsend[y, 0].astype(F32) if c == 0 else qrecv[1, 0].astype(F32)
        for k in range(1, ny):
            rows_q += qrecv[c, k].astype(F32)
        gq_ref[:, lanes_out] = jnp.transpose(rows_q * SCALE).astype(BF16)
    for c, lanes_out in ((1, other_lanes), (0, own_lanes)):
        part_v = finv_in[...] if c == 1 else acc_v[0, pl.ds(0, T), :]
        part_k = fink_in[...].astype(F32) if c == 1 else acc_k[0, pl.ds(0, T), :]
        for way in (0, 1) if c == 1 else (1, 0):
            for t, (first, count, acc, src, to) in enumerate(pieces):
                arrived(to.at[way, half - 1, c, pl.ds(first, count)], rs_r.at[t, way, half - 1, c])
            part_v += rsv_in[way, half - 1, c]
            part_k += rsk_in[way, half - 1, c].astype(F32)
        gv_ref[:, lanes_out] = part_v.astype(BF16)
        gk_ref[:, lanes_out] = (part_k * SCALE).astype(BF16)

    for k in range(1, nz):
        arrived(grecv.at[k], g_r.at[k])
    weight_rows = gsend[z]
    for k in range(1, nz):
        weight_rows += grecv[k]
    gw_ref[...] = weight_rows

    for copy in started:
        copy.wait_send()


def shards(ny, nz, queries, keys, values, out_grad, w_out, frame_index, group_order):
    half = nz // 2
    width = out_grad.shape[1]
    cols = width // (2 * ny)
    zcols = cols // nz
    pairs = group_order.shape[0] // 2
    frames_in = frame_index.reshape(pairs, T)
    order_in = group_order.reshape(1, 2 * pairs)
    vmem = pltpu.VMEM
    dma = pltpu.SemaphoreType.DMA
    any_spec = pl.BlockSpec(memory_space=pltpu.HBM)
    out_spec = pl.BlockSpec(memory_space=pltpu.VMEM)
    results = pl.pallas_call(
        functools.partial(kernel, ny, nz),
        out_shape=(
            jax.ShapeDtypeStruct((T, 6 * HD), BF16),
            jax.ShapeDtypeStruct((zcols, 2 * HD), F32),
        ),
        in_specs=[any_spec] * 7,
        out_specs=(out_spec,) * 2,
        scratch_shapes=[
            vmem((T, 2 * HD), BF16),
            vmem((T, 2 * HD), BF16),
            vmem((T, 2 * HD), BF16),
            vmem((T, width), BF16),
            vmem((2 * HD, width), BF16),
            vmem((pairs, T), jnp.int32),
            vmem((1, 2 * pairs), jnp.int32),
            vmem((T, 2 * HD), BF16),
            vmem((2, T, HD), BF16),
            vmem((2, T, HD), BF16),
            vmem((nz, 2, 2, T, HD), BF16),
            vmem((ny, 2, 2, T, HD), BF16),
            vmem((pairs, T), F32),
            vmem((nz, B, T), F32),
            vmem((ny, B), F32),
            vmem((nz, ny, B, B), F32),
            vmem((nz, ny, B, B), F32),
            vmem((nz, HD, B), BF16),
            vmem((nz, ny, B), F32),
            vmem((nz, ny, B), F32),
            vmem((nz, ny, B), F32),
            vmem((ny, 3, ny, B), F32),
            vmem((nz, ny, B), F32),
            vmem((ny, ny, B), F32),
            vmem((ny, B), F32),
            vmem((ny, HD, B), BF16),
            vmem((ny, HD, B), BF16),
            vmem((2, ny, HD, B), BF16),
            vmem((ny, 2, T, cols), BF16),
            vmem((nz, zcols, 2 * HD), F32),
            vmem((nz, zcols, 2 * HD), F32),
            vmem((nz, B, HD), F32),
            vmem((nz, B, HD), F32),
            vmem((ny, HD, B), F32),
            vmem((2, half, 2, T, HD), BF16),
            vmem((2, half, 2, T, HD), BF16),
            vmem((2, half, 2, T, HD), F32),
            vmem((2, half, 2, T, HD), F32),
            vmem((ny, 2, HD, T), BF16),
            vmem((2, ny, HD, T), BF16),
            vmem((T, HD), F32),
            vmem((T, HD), F32),
            vmem((T, HD), BF16),
            vmem((T, HD), BF16),
            dma((7,)),
            dma((160,)),
            dma((nz, 2)),
            dma((ny, 2)),
            dma((2, ny)),
            dma((ny,)),
            dma((ny,)),
            dma((2, ny)),
            dma((nz,)),
            dma((3, 2, half, 2)),
            dma((2, ny)),
            dma((2,)),
        ],
        compiler_params=pltpu.CompilerParams(
            collective_id=0, has_side_effects=True, vmem_limit_bytes=63 * 1024 * 1024
        ),
    )(queries, keys, values, out_grad, w_out, frames_in, order_in)
    o, g = results
    return o[:, :B], o[:, B:2*B], o[:, 2*B:], jnp.transpose(g)


def solution(mesh):
    ny, nz = {64: (4, 8), 32: (2, 8), 16: (2, 4)}[mesh.shape["ctx"]]
    placed = (
        P("ctx", "tp"),
        P("ctx", "tp"),
        P("ctx", "tp"),
        P("ctx", None),
        P("tp", None),
        P(),
        P(),
    )
    return jax.shard_map(
        functools.partial(shards, ny, nz),
        mesh=mesh,
        in_specs=placed,
        out_specs=(P("ctx", "tp"), P("ctx", "tp"), P("ctx", "tp"), P("tp", "ctx")),
        check_vma=False,
    )
```
